32 devices in a mesh: slab: 4 (over y, x), plane: 8 (over z, core).
Axes of the slice: x: 2, y: 2, z: 4, core: 2. Of those that a mesh axis runs over, the one named last changes fastest.
Arguments:
- images: float32 [2, 32, 128, 1024], P(None, 'slab', 'plane'), may hold values from -12 to 12, as said below
- shifts: int32 [3, 4, 16, 128], P(None, 'slab', 'plane'), may hold values from -1 to 1
- initial_displacement: float32 [3, 4, 16, 128], P(None, 'slab', 'plane'), may hold values from -2 to 2
Outputs:
- displacement: float32 [3, 4, 16, 128], P(None, 'slab', 'plane')
- mismatch: float32 [32, 128, 1024], P('slab', 'plane')
The draws below stay inside these ranges and needn't reach their ends.
Inputs may be any that keep to these rules, and one draw needn't show every extreme that they name: `images`: voxel intensities.
All inputs are finite; a program needn't handle non-finite values.
Results may differ from the reference program's by a relative error of at most 0.0023.
Values sent between devices are 32-bit elements; how exact they have to be, the bound alone decides.
A program may use at most 192 MiB of HBM per device.

```python
import jax
import jax.numpy as jnp

ELEM = 8
ITERS = 6
NX = 1024
NZ = 32
NY = 128
ELEMENT_LAYERS = 4
ELEMENT_ROWS = 16
ELEMENTS_ACROSS = 128


def draw_images(key, part):
    depth_frac = (jnp.arange(NZ, dtype=jnp.float32) + 0.5) / NZ
    height_frac = (jnp.arange(NY, dtype=jnp.float32) + 0.5) / NY
    noise = jnp.clip(jax.random.normal(key, (2, NZ, NY, NX), jnp.float32), -4.0, 4.0)
    scales = 3.0 ** (depth_frac[:, None] + height_frac[None, :]) / 3.0
    return scales[None, :, :, None] * noise


def place_ends(values, key, low, top_value):
    shape = values.shape
    index_at = [jax.random.randint(jax.random.fold_in(key, axis), (), 0, shape[axis]) for axis in range(len(shape))]
    values = values.at[tuple(index_at)].set(low)
    longest = shape.index(max(shape))
    index_at[longest] = (index_at[longest] + 1) % shape[longest]
    return values.at[tuple(index_at)].set(top_value)


def block_scale(rng, shape, cuts, low, largest):
    level = 1.0
    for position, blocks in cuts:
        draws = jax.random.uniform(jax.random.fold_in(jax.random.fold_in(rng, 6), position), (blocks,), jnp.float32, low / len(cuts), largest / len(cuts))
        level = level * jnp.repeat(jnp.exp(draws), shape[position] // blocks).reshape((-1,) + (1,) * (len(shape) - 1 - position))
    return level


def gaussian(own_key, dims, deviation, bound, pieces=(), kind=jnp.bfloat16):
    values = jax.random.normal(own_key, dims, jnp.float32) * deviation
    if len(pieces) > 0:
        values = block_scale(own_key, dims, pieces, -0.22, 0.18) * values
    return jnp.clip(values, min=-bound, max=bound).astype(kind)


def setup_inputs(seed: int = 0) -> dict:
    splits = jax.random.split(jax.random.key(seed), 4)
    return {
        "images": draw_images(jax.random.fold_in(splits[3], 71), 0),
        "shifts": place_ends(jax.random.randint(splits[1], (3, ELEMENT_LAYERS, ELEMENT_ROWS, ELEMENTS_ACROSS), -1, 2), jax.random.fold_in(splits[1], 1), -1, 1).astype(jnp.int32),
        "initial_displacement": gaussian(splits[2], (3, ELEMENT_LAYERS, ELEMENT_ROWS, ELEMENTS_ACROSS), 0.3, 2.0, ((1, 4), (2, 8)), jnp.float32),
    }


reg_weight = 4.0


def edge_weights():
    return jnp.arange(ELEM, dtype=jnp.float32) / ELEM


def interpolate(padded):
    weights = edge_weights()
    lower_w = 1.0 - weights
    comps, nodes_z, nodes_y, nodes_x = padded.shape
    depth_direction = padded[:, :-1, None] * lower_w[:, None, None] + padded[:, 1:, None] * weights[:, None, None]
    depth_direction = depth_direction.reshape(comps, (nodes_z - 1) * ELEM, nodes_y, nodes_x)
    along_y = depth_direction[:, :, :-1, None] * lower_w[:, None] + depth_direction[:, :, 1:, None] * weights[:, None]
    along_y = along_y.reshape(comps, (nodes_z - 1) * ELEM, (nodes_y - 1) * ELEM, nodes_x)
    along_x = along_y[..., :-1, None] * lower_w + along_y[..., 1:, None] * weights
    return along_x.reshape(comps, (nodes_z - 1) * ELEM, (nodes_y - 1) * ELEM, (nodes_x - 1) * ELEM)


def laplacian(padded):
    centre = padded[:, 1:-1, 1:-1, 1:-1]
    beside = padded[:, :-2, 1:-1, 1:-1] + padded[:, 2:, 1:-1, 1:-1]
    beside = beside + padded[:, 1:-1, :-2, 1:-1] + padded[:, 1:-1, 2:, 1:-1]
    beside = beside + padded[:, 1:-1, 1:-1, :-2] + padded[:, 1:-1, 1:-1, 2:]
    return 6.0 * centre - beside


def collapse_width(field):
    weights = edge_weights()
    comps, zcount, ycount, xcount = field.shape
    blocks = field.reshape(comps, zcount, ycount, xcount // ELEM, ELEM)
    lower = jnp.sum(blocks * (1.0 - weights), -1)
    upper = jnp.sum(blocks * weights, -1)
    return lower + jnp.concatenate([jnp.zeros_like(upper[..., :1]), upper[..., :-1]], -1)


def reduce_y(field):
    weights = edge_weights()
    comps, zcount, ycount, xcount = field.shape
    blocks = field.reshape(comps, zcount, ycount // ELEM, ELEM, xcount)
    lower = jnp.sum(blocks * (1.0 - weights)[:, None], 3)
    upper = jnp.sum(blocks * weights[:, None], 3)
    return lower, upper


def reduce_z(field):
    weights = edge_weights()
    comps, zcount, ycount, xcount = field.shape
    blocks = field.reshape(comps, zcount // ELEM, ELEM, ycount, xcount)
    lower = jnp.sum(blocks * (1.0 - weights)[:, None, None], 2)
    upper = jnp.sum(blocks * weights[:, None, None], 2)
    return lower, upper


def restrict(field):
    nodes_x = collapse_width(field)
    lower, upper = reduce_y(nodes_x)
    nodes_y = lower + jnp.concatenate([jnp.zeros_like(upper[:, :, :1]), upper[:, :, :-1]], 2)
    lower, upper = reduce_z(nodes_y)
    return lower + jnp.concatenate([jnp.zeros_like(upper[:, :1]), upper[:, :-1]], 1)


def gradient(padded, margin, zcount, ycount, xcount):
    def piece(off_z, off_y, off_x):
        return padded[margin + off_z:margin + off_z + zcount, margin + off_y:margin + off_y + ycount, margin + off_x:margin + off_x + xcount]

    grad_z = (piece(-2, 0, 0) - 8.0 * piece(-1, 0, 0) + 8.0 * piece(1, 0, 0) - piece(2, 0, 0)) / 12.0
    gradient_height = (piece(0, -2, 0) - 8.0 * piece(0, -1, 0) + 8.0 * piece(0, 1, 0) - piece(0, 2, 0)) / 12.0
    grad_x = (piece(0, 0, -2) - 8.0 * piece(0, 0, -1) + 8.0 * piece(0, 0, 1) - piece(0, 0, 2)) / 12.0
    return jnp.stack([grad_z, gradient_height, grad_x])


def voxel_codes(shifts):
    codes = (shifts[0] + 1) * 9 + (shifts[1] + 1) * 3 + (shifts[2] + 1)
    elem_z, elem_y, elem_x = codes.shape
    spread = jnp.broadcast_to(codes[:, None, :, None, :, None], (elem_z, ELEM, elem_y, ELEM, elem_x, ELEM))
    return spread.reshape(elem_z * ELEM, elem_y * ELEM, elem_x * ELEM).astype(jnp.int32)


def warp_image(padded, margin, codes):
    zcount, ycount, xcount = codes.shape
    result = jnp.zeros(codes.shape, padded.dtype)
    for candidate in range(27):
        off_z = candidate // 9 - 1
        off_y = (candidate // 3) % 3 - 1
        off_x = candidate % 3 - 1
        piece = padded[margin + off_z:margin + off_z + zcount, margin + off_y:margin + off_y + ycount, margin + off_x:margin + off_x + xcount]
        result = jnp.where(codes == candidate, piece, result)
    return result


def reference(images, shifts, initial_displacement):
    ref_img = images[0]
    codes = voxel_codes(shifts)
    grads = gradient(jnp.pad(ref_img, 2), 2, NZ, NY, NX)
    warped = warp_image(jnp.pad(images[1], 1), 1, codes)
    node_pad = jnp.pad(initial_displacement, ((0, 0), (1, 1), (1, 1), (1, 1)))
    moved = interpolate(node_pad[:, 1:, 1:, 1:])
    mismatch = ref_img - warped - jnp.sum(grads * moved, 0)
    energy = jnp.sum(grads * grads)
    smoothing_penalty = reg_weight * energy / (NZ * NY * NX)

    def apply_op(vector):
        vector_pad = jnp.pad(vector, ((0, 0), (1, 1), (1, 1), (1, 1)))
        flow = interpolate(vector_pad[:, 1:, 1:, 1:])
        scalar = jnp.sum(grads * flow, 0)
        return restrict(grads * scalar[None]) + smoothing_penalty * laplacian(vector_pad)

    rhs = restrict(grads * mismatch[None]) - smoothing_penalty * laplacian(node_pad)
    step = jnp.zeros_like(rhs)
    residual = rhs
    direction = rhs
    norm_now = jnp.sum(residual * residual)
    for sweep in range(ITERS):
        applied = apply_op(direction)
        step_size = norm_now / jnp.sum(direction * applied)
        step = step + step_size * direction
        residual = residual - step_size * applied
        norm_next = jnp.sum(residual * residual)
        direction = residual + (norm_next / norm_now) * direction
        norm_now = norm_next
    return initial_displacement + step, mismatch
```

```python
import functools

import jax
import jax.numpy as jnp
import ml_dtypes
import numpy as np
from jax import lax
from jax.experimental import pallas as pl
from jax.experimental.pallas import tpu as pltpu
from jax.sharding import PartitionSpec as P

ITERS = 6
reg_weight = 4.0

MESH = pl.DeviceIdType.MESH
F32 = jnp.float32
BF16 = jnp.bfloat16
TILE = 8
COMPS = 3
PAIRS = ((0, 0), (0, 1), (0, 2), (1, 1), (1, 2), (2, 2))
AROUND = tuple((dz, dy) for dz in (-1, 0, 1) for dy in (-1, 0, 1) if (dz, dy) != (0, 0))


def place_of(dz, dy):
    return (dz + 1) * 3 + dy + 1


def pair_of(i, j):
    return PAIRS.index((min(i, j), max(i, j)))


def matrices(elem, rows, across):
    w = np.arange(elem) / elem
    squares = ((1 - w) ** 2, w * (1 - w), w**2)
    count = elem * across
    hats = np.zeros((count, across))
    stencil = np.zeros((count, 2 * across))
    spread = np.zeros((across, count))
    for e in range(across):
        at = slice(e * elem, (e + 1) * elem)
        spread[e, at] = 1
        hats[at, e] = 1 - w
        stencil[at, e] += squares[0]
        if e + 1 < across:
            hats[at, e + 1] = w
            stencil[at, e + 1] += squares[2]
            stencil[at, across + e] = squares[1]

    height = rows * elem
    depth = len(PAIRS) * 3 * height

    def column(ij, cz, row):
        start = (ij * 3 + cz) * height + row * elem
        return slice(start, start + elem)

    last = rows - 1
    slab_rows = [(ij, cz, cy, r) for ij in range(6) for cz in (1, 2) for cy in range(3) for r in range(rows)]
    plane_rows = [(ij, cz, cy, last) for ij in range(6) for cz in (0, 1) for cy in (1, 2)]
    diag_rows = [(ij, cz, cy, last) for ij in range(6) for cz in (1, 2) for cy in (1, 2)]
    parts = []
    start = 0
    for listed in (slab_rows, plane_rows, diag_rows):
        used = -(-len(listed) // TILE) * TILE
        parts.append((start, used))
        start += used + TILE
    total = start
    send = np.zeros((total, depth))
    index = [{}, {}, {}]
    for part, listed in enumerate((slab_rows, plane_rows, diag_rows)):
        for n, key in enumerate(listed):
            ij, cz, cy, r = key
            send[parts[part][0] + n, column(ij, cz, r)] = squares[cy]
            index[part][key] = parts[part][0] + n

    own = np.zeros((COMPS * 9 * TILE, depth))
    came = np.zeros((COMPS * 9 * TILE, total))
    for i in range(COMPS):
        for dz in (-1, 0, 1):
            for dy in (-1, 0, 1):
                for j in range(COMPS):
                    for r in range(rows):
                        out = (i * 9 + place_of(dz, dy)) * TILE + j * rows + r
                        ij = pair_of(i, j)
                        layers = {0: ((0, 0), (-1, 2)), 1: ((0, 1),), -1: ((-1, 1),)}[dz]
                        lines = {0: ((r, 0), (r - 1, 2)), 1: ((r, 1),), -1: ((r - 1, 1),)}[dy]
                        for layer, cz in layers:
                            for line, cy in lines:
                                if layer == 0 and line >= 0:
                                    own[out, column(ij, cz, line)] = squares[cy]
                                elif layer < 0 and line >= 0:
                                    came[out, index[0][(ij, cz, cy, line)]] = 1
                                elif layer == 0:
                                    came[out, index[1][(ij, cz, cy, last)]] = 1
                                else:
                                    came[out, index[2][(ij, cz, cy, last)]] = 1

    loads = np.zeros((4 * TILE, COMPS * 2 * height))

    def line_of(i, cz, row):
        start = (i * 2 + cz) * height + row * elem
        return slice(start, start + elem)

    for i in range(COMPS):
        for r in range(rows):
            out = i * rows + r
            for cz in (0, 1):
                loads[cz * TILE + out, line_of(i, cz, r)] = 1 - w
                if r > 0:
                    loads[cz * TILE + out, line_of(i, cz, r - 1)] = w
        for cz in (0, 1):
            loads[(2 + cz) * TILE + i * rows, line_of(i, cz, last)] = w
    arrays = (stencil, hats, hats.T, spread, send, own, came, loads)
    return parts, [np.asarray(a, dtype=ml_dtypes.bfloat16) for a in arrays]


def split(x):
    high = x.astype(BF16)
    return high, (x - high.astype(F32)).astype(BF16)


def dot(a, b):
    return jnp.dot(a, b, preferred_element_type=F32)


def dot_left(x, exact):
    high, low = split(x)
    return dot(high, exact) + dot(low, exact)


def dot_right(exact, x):
    high, low = split(x)
    return dot(exact, high) + dot(exact, low)


def kernel(
    slabs,
    planes,
    parts,
    images,
    shifts,
    start_field,
    w_stencil,
    w_hats,
    w_nodes,
    w_spread,
    w_send,
    w_own,
    w_came,
    w_loads,
    out_field,
    out_mismatch,
    ref_ext,
    def_ext,
    pack,
    got_rows,
    got_diag,
    tiles,
    halo,
    dots,
    grads,
    mis,
    nodes_x,
    moves,
    moments,
    loads,
    send_buf,
    got_buf,
    coefs,
    res,
    img,
    load_sem,
    out_sem,
    face_send,
    face_recv,
    row_send,
    row_recv,
    diag_send,
    diag_recv,
    tile_send,
    tile_recv,
    dot_send,
    dot_recv,
    part_send,
    part_recv,
):
    _, zs, ys, xs = images.shape
    rows, across = shifts.shape[2], shifts.shape[3]
    elem = xs // across
    devices = slabs * planes
    slab, plane = lax.axis_index("slab"), lax.axis_index("plane")
    me = slab * planes + plane

    def present(dz, dy):
        ok = None
        for d, at, count in ((dz, slab, slabs), (dy, plane, planes)):
            if d:
                here = at < count - 1 if d > 0 else at > 0
                ok = here if ok is None else jnp.logical_and(ok, here)
        return ok

    def beside(dz, dy):
        return (slab + dz, plane + dy)

    def other(k):
        to = lax.rem(me + k, devices)
        return (lax.div(to, planes), lax.rem(to, planes))

    mine = [
        pltpu.make_async_copy(images.at[0], ref_ext.at[pl.ds(2, zs), pl.ds(TILE, ys)], load_sem.at[0]),
        pltpu.make_async_copy(images.at[1], def_ext.at[pl.ds(1, zs), pl.ds(TILE, ys)], load_sem.at[1]),
    ]
    for copy in mine:
        copy.start()
    halo[...] = jnp.zeros(halo.shape, F32)
    tiles[...] = jnp.zeros(tiles.shape, F32)
    got_buf[...] = jnp.zeros(got_buf.shape, F32)
    for j in range(COMPS):
        tiles[0, j * rows : (j + 1) * rows, :] = start_field[j, 0]

    barrier = pltpu.get_barrier_semaphore()

    def greet(k, carry):
        pl.semaphore_signal(barrier, inc=1, device_id=other(k), device_id_type=MESH)
        return carry

    lax.fori_loop(1, devices, greet, 0)
    for copy in mine:
        copy.wait()

    for side, (far, near) in enumerate(((1, 0), (ys - 2, ys - 1))):
        pack[side, 0:zs, :] = ref_ext[2 : 2 + zs, TILE + far, :]
        pack[side, zs : 2 * zs, :] = ref_ext[2 : 2 + zs, TILE + near, :]
        pack[side, 2 * zs :, :] = def_ext[1 : 1 + zs, TILE + near, :]
    pl.semaphore_wait(barrier, devices - 1)

    def remote(src, dst, send, recv, to):
        return pltpu.make_async_remote_copy(
            src_ref=src, dst_ref=dst, send_sem=send, recv_sem=recv, device_id=to, device_id_type=MESH
        )

    def faces():
        out = []
        for n, d in enumerate((-1, 1)):
            low = 0 if d < 0 else zs - 2
            here = ref_ext.at[pl.ds(2 + low, 2), pl.ds(TILE, ys)]
            there = ref_ext.at[pl.ds(2 + zs if d < 0 else 0, 2), pl.ds(TILE, ys)]
            out.append(((d, 0), remote(here, there, face_send.at[n, 0], face_recv.at[n, 0], beside(d, 0))))
            low = 0 if d < 0 else zs - 1
            here = def_ext.at[pl.ds(1 + low, 1), pl.ds(TILE, ys)]
            there = def_ext.at[pl.ds(1 + zs if d < 0 else 0, 1), pl.ds(TILE, ys)]
            out.append(((d, 0), remote(here, there, face_send.at[n, 1], face_recv.at[n, 1], beside(d, 0))))
        for n, d in enumerate((-1, 1)):
            out.append(
                ((0, d), remote(pack.at[n], got_rows.at[n], row_send.at[n], row_recv.at[n], beside(0, d)))
            )
        for n, (dz, dy) in enumerate(((-1, -1), (-1, 1), (1, -1), (1, 1))):
            here = pack.at[(dy + 1) // 2, pl.ds(2 * zs, zs)]
            out.append(
                ((dz, dy), remote(here, got_diag.at[n], diag_send.at[n], diag_recv.at[n], beside(dz, dy)))
            )
        return out

    def around(stage):
        out = []
        for n, (dz, dy) in enumerate(AROUND):
            copy = remote(
                tiles.at[stage],
                halo.at[stage, place_of(-dz, -dy)],
                tile_send.at[stage, n],
                tile_recv.at[stage, n],
                beside(dz, dy),
            )
            out.append(((dz, dy), copy))
        return out

    def begin(copies):
        for (dz, dy), copy in copies:
            pl.when(present(dz, dy))(copy.start)

    def arrive(copies):
        for (dz, dy), copy in copies:
            pl.when(present(-dz, -dy))(copy.wait_recv)

    def sent(copies):
        for (dz, dy), copy in copies:
            pl.when(present(dz, dy))(copy.wait_send)

    def share(stage):
        def one(k, carry):
            slot = dots.at[stage, me]
            remote(slot, slot, dot_send.at[stage], dot_recv.at[stage], other(k)).start()
            return carry

        lax.fori_loop(1, devices, one, 0)

    def shared(sem, stage):
        some = dots.at[stage, pl.ds(0, devices - 1)]
        pltpu.make_async_copy(some, some, sem.at[stage]).wait()

    def totals(stage):
        shared(dot_recv, stage)
        lanes = jnp.sum(dots[stage], axis=0)
        return jnp.sum(lanes, axis=1, keepdims=True)

    image_copies = faces()
    start_copies = around(0)
    begin(image_copies)
    begin(start_copies)

    codes = jnp.concatenate([shifts[j, 0] for j in range(COMPS)], axis=0).astype(F32).astype(BF16)
    wide = dot(codes, w_spread[...])
    for n, dx in enumerate((-1, 0, 1)):
        moves[n, 0 : COMPS * rows, :] = pltpu.roll(wide, dx % xs, 1) if dx else wide

    arrive(start_copies)
    halo[0, place_of(0, 0)] = tiles[0]
    corner = jnp.concatenate([halo[0, place_of(dz, dy)] for dz in (0, 1) for dy in (0, 1)], axis=0)
    nodes_x[...] = dot_left(corner, w_nodes[...])

    arrive(image_copies)

    def clear(dz, dy, *views):
        def run():
            for ref, index in views:
                ref[index] = jnp.zeros(ref[index].shape, F32)

        pl.when(jnp.logical_not(present(dz, dy)))(run)

    clear(-1, 0, (ref_ext, (slice(0, 2),)), (def_ext, (slice(0, 1),)))
    clear(1, 0, (ref_ext, (slice(2 + zs, 4 + zs),)), (def_ext, (slice(1 + zs, 2 + zs),)))
    for n, d in enumerate((1, -1)):
        clear(0, d, (got_rows, (n,)))
    for n, (dz, dy) in enumerate(((1, 1), (1, -1), (-1, 1), (-1, -1))):
        clear(dz, dy, (got_diag, (n,)))
    top = TILE + ys
    ref_ext[2 : 2 + zs, top, :] = got_rows[0, zs : 2 * zs, :]
    ref_ext[2 : 2 + zs, top + 1, :] = got_rows[0, 0:zs, :]
    def_ext[1 : 1 + zs, top, :] = got_rows[0, 2 * zs :, :]
    ref_ext[2 : 2 + zs, TILE - 2, :] = got_rows[1, 0:zs, :]
    ref_ext[2 : 2 + zs, TILE - 1, :] = got_rows[1, zs : 2 * zs, :]
    def_ext[1 : 1 + zs, TILE - 1, :] = got_rows[1, 2 * zs :, :]
    def_ext[1 + zs, top : top + 1, :] = got_diag[0, 0:1, :]
    def_ext[1 + zs, TILE - 1 : TILE, :] = got_diag[1, 0:1, :]
    def_ext[0, top : top + 1, :] = got_diag[2, zs - 1 : zs, :]
    def_ext[0, TILE - 1 : TILE, :] = got_diag[3, zs - 1 : zs, :]

    lane = lax.broadcasted_iota(jnp.int32, (TILE, xs), 1)
    up = lax.broadcasted_iota(jnp.int32, (TILE, xs), 0).astype(F32) / elem

    def along(value, d):
        rolled = pltpu.roll(value, (-d) % xs, 1)
        inside = lane < xs - d if d > 0 else lane >= -d
        return jnp.where(inside, rolled, 0.0)

    def voxels(z, energy):
        wz = z.astype(F32) / elem
        for r in range(rows):
            base = TILE + r * elem

            def ref(dz, dy):
                return ref_ext[z + (2 + dz), base + dy : base + dy + elem, :]

            centre = ref(0, 0)
            g = [
                (ref(-2, 0) - ref(2, 0) + 8.0 * (ref(1, 0) - ref(-1, 0))) * (1.0 / 12.0),
                (ref(0, -2) - ref(0, 2) + 8.0 * (ref(0, 1) - ref(0, -1))) * (1.0 / 12.0),
                (
                    along(centre, -2)
                    - along(centre, 2)
                    + 8.0 * (along(centre, 1) - along(centre, -1))
                )
                * (1.0 / 12.0),
            ]
            warped = None
            for n, dx in enumerate((-1, 0, 1)):
                s = [moves[n, j * rows + r : j * rows + r + 1, :] for j in range(2)]
                s = [jnp.broadcast_to(v, (elem, xs)) for v in s]
                below, above = s[0] < -0.5, s[0] > 0.5
                line = []
                for dy in (-1, 0, 1):
                    at = pl.ds(base + dy, elem)
                    value = jnp.where(below, def_ext[z, at, :], def_ext[z + 1, at, :])
                    line.append(jnp.where(above, def_ext[z + 2, at, :], value))
                value = jnp.where(s[1] < -0.5, line[0], line[1])
                value = jnp.where(s[1] > 0.5, line[2], value)
                if dx:
                    value = along(value, dx)
                sx = jnp.broadcast_to(moves[1, 2 * rows + r : 2 * rows + r + 1, :], (elem, xs))
                if warped is None:
                    warped = value
                else:
                    warped = jnp.where(sx > dx - 0.5, value, warped)
            total = centre - warped
            for j in range(COMPS):

                def node(line):
                    dy = line // rows
                    at = j * rows + line % rows
                    low = nodes_x[dy * TILE + at : dy * TILE + at + 1, :]
                    high = nodes_x[(2 + dy) * TILE + at : (2 + dy) * TILE + at + 1, :]
                    return (1.0 - wz) * low + wz * high

                moved = (1.0 - up) * node(r) + up * node(r + 1)
                total = total - g[j] * moved
                grads[j, z, r * elem : (r + 1) * elem, :] = g[j]
                energy = energy + g[j] * g[j]
            mis[z, r * elem : (r + 1) * elem, :] = total
        return energy

    energy = lax.fori_loop(0, zs, voxels, jnp.zeros((TILE, xs), F32))
    store = pltpu.make_async_copy(mis, out_mismatch, out_sem)
    store.start()
    energy = jnp.sum(energy, axis=0, keepdims=True)
    dots[0, me] = jnp.zeros(dots.shape[2:], F32)
    row = energy[:, :across]
    for c in range(1, xs // across):
        row = row + energy[:, c * across : (c + 1) * across]
    dots[0, me, 0:1, :] = row
    share(0)

    width = 128
    lines = xs // width

    def gather(n, carry):
        r, c = lax.div(n, lines), lax.rem(n, lines)
        ay = pl.ds(pl.multiple_of(r * elem, elem), elem)
        ax = pl.ds(pl.multiple_of(c * width, width), width)
        sums = [[None] * 3 for _ in PAIRS]
        forces = [[None] * 2 for _ in range(COMPS)]

        def add(total, weight, value):
            if weight == 0.0:
                return total
            term = value if weight == 1.0 else weight * value
            return term if total is None else total + term

        for z in range(zs):
            w = z / elem
            g = [grads[j, z, ay, ax] for j in range(COMPS)]
            q = mis[z, ay, ax]
            for ij, (i, j) in enumerate(PAIRS):
                product = g[i] * g[j]
                for cz, weight in enumerate(((1 - w) ** 2, w * (1 - w), w * w)):
                    sums[ij][cz] = add(sums[ij][cz], weight, product)
            for i in range(COMPS):
                product = g[i] * q
                for cz, weight in enumerate((1 - w, w)):
                    forces[i][cz] = add(forces[i][cz], weight, product)
        for ij in range(len(PAIRS)):
            for cz in range(3):
                at = pl.multiple_of((ij * 3 + cz) * ys + r * elem, elem)
                moments[pl.ds(at, elem), ax] = sums[ij][cz]
        for i in range(COMPS):
            for cz in range(2):
                at = pl.multiple_of((i * 2 + cz) * ys + r * elem, elem)
                loads[pl.ds(at, elem), ax] = forces[i][cz]
        return carry

    lax.fori_loop(0, rows * lines, gather, 0)
    summed = dot_left(moments[...], w_stencil[...])
    load_tiles = dot_right(w_loads[...], dot_left(loads[...], w_hats[...]))
    send_buf[...] = dot_right(w_send[...], summed)
    for (start, used), n in zip(parts, (1, 2, 3)):
        send_buf[start + used : start + used + TILE, :across] = load_tiles[n * TILE : (n + 1) * TILE]
    part_copies = []
    for n, ((start, used), to) in enumerate(zip(parts, ((1, 0), (0, 1), (1, 1)))):
        at = pl.ds(start, used + TILE)
        part_copies.append(
            (to, remote(send_buf.at[at], got_buf.at[at], part_send.at[n], part_recv.at[n], beside(*to)))
        )
    begin(part_copies)
    coefs[...] = dot_right(w_own[...], summed)

    node_lane = lax.broadcasted_iota(jnp.int32, (TILE, across), 1)
    sub = lax.broadcasted_iota(jnp.int32, (TILE, across), 0)
    line = lax.rem(sub, rows)
    group = lax.div(sub, rows)

    def neighbour(get, dz, dy):
        centre = get(place_of(dz, 0))
        if dy == 0:
            return centre
        edge = get(place_of(dz, dy))
        inner = pltpu.roll(centre, (-dy) % TILE, 0)
        outer = pltpu.roll(edge, (dy * (rows - 1)) % TILE, 0)
        return jnp.where(line == (rows - 1 if dy > 0 else 0), outer, inner)

    def start_at(place):
        return halo[0, place]

    centre = start_at(place_of(0, 0))
    lap = 6.0 * centre - neighbour(start_at, -1, 0) - neighbour(start_at, 1, 0)
    lap = lap - neighbour(start_at, 0, -1) - neighbour(start_at, 0, 1)
    lap = lap - jnp.where(node_lane > 0, pltpu.roll(centre, 1, 1), 0.0)
    lap = lap - jnp.where(node_lane < across - 1, pltpu.roll(centre, across - 1, 1), 0.0)
    lap = jnp.where(group < COMPS, lap, 0.0)

    penalty = totals(0)[0:1, :] * (reg_weight / (devices * zs * ys * xs))
    arrive(part_copies)
    rhs = load_tiles[0:TILE] - penalty * lap
    for start, used in parts:
        rhs = rhs + got_buf[start + used : start + used + TILE, :across]
    tiles[1] = rhs
    rhs_copies = around(1)
    begin(rhs_copies)

    coefs[...] = coefs[...] + dot_right(w_came[...], got_buf[...])
    for i in range(COMPS):
        same = jnp.where(group == i, 1.0, 0.0) * penalty

        def raise_by(dz, dy, part, value):
            at = pl.ds((i * 9 + place_of(dz, dy)) * TILE, TILE)
            to = pl.ds(part * across, across)
            coefs[at, to] = coefs[at, to] + value

        raise_by(0, 0, 0, 6.0 * same)
        raise_by(0, 0, 1, jnp.where(node_lane < across - 1, -same, 0.0))
        for dz, dy in ((-1, 0), (1, 0), (0, -1), (0, 1)):
            raise_by(dz, dy, 0, -same)

    arrive(rhs_copies)
    halo[1, place_of(0, 0)] = rhs
    res[...] = halo[1]
    img[...] = jnp.zeros(img.shape, F32)

    def operate():
        out = [None] * COMPS
        back = [None] * COMPS
        for dz in (-1, 0, 1):
            for dy in (-1, 0, 1):
                v = neighbour(lambda place: res[place], dz, dy)
                ahead = pltpu.roll(v, across - 1, 1)
                for i in range(COMPS):
                    at = pl.ds((i * 9 + place_of(dz, dy)) * TILE, TILE)
                    here, link = coefs[at, 0:across], coefs[at, across : 2 * across]
                    term = here * v + link * ahead
                    out[i] = term if out[i] is None else out[i] + term
                    term = link * v
                    back[i] = term if back[i] is None else back[i] + term
        image = jnp.zeros((TILE, across), F32)
        for i in range(COMPS):
            value = out[i] + pltpu.roll(back[i], 1, 1)
            value = value + pltpu.roll(value, TILE // 2, 0)
            value = value + pltpu.roll(value, rows, 0)
            image = jnp.where(group == i, value, image)
        return image

    direction = jnp.zeros((TILE, across), F32)
    step = jnp.zeros((TILE, across), F32)
    norm_before = size_before = None
    copies = [image_copies, start_copies, part_copies, rhs_copies]
    for k in range(ITERS):
        image = operate()
        residual = res[place_of(0, 0)]
        stage = k + 1
        dots[stage, me, 0:1, :] = jnp.sum(residual * residual, axis=0, keepdims=True)
        dots[stage, me, 1:2, :] = jnp.sum(residual * image, axis=0, keepdims=True)
        share(stage)
        if k < ITERS - 1:
            tiles[stage + 1] = image
            halo_copies = around(stage + 1)
            begin(halo_copies)
            copies.append(halo_copies)
        sums = totals(stage)
        norm, inner = sums[0:1, :], sums[1:2, :]
        if k == 0:
            size = norm / inner
            direction = residual
        else:
            ratio = norm / norm_before
            size = norm / (inner - ratio * norm / size_before)
            direction = residual + ratio * direction
        step = step + size * direction
        norm_before, size_before = norm, size
        if k < ITERS - 1:
            arrive(halo_copies)
            halo[stage + 1, place_of(0, 0)] = image
            flow = halo[stage + 1]
            if k > 0:
                flow = flow + ratio * img[...]
            img[...] = flow
            res[...] = res[...] - size * flow

    result = tiles[0] + step
    for j in range(COMPS):
        out_field[j, 0] = result[j * rows : (j + 1) * rows]
    for listed in copies:
        sent(listed)
    for stage in range(ITERS + 1):
        shared(dot_send, stage)
    store.wait()


def body(slabs, planes, images, shifts, initial_displacement):
    _, zs, ys, xs = images.shape
    layers, rows, across = shifts.shape[1:]
    elem = xs // across
    assert layers == 1 and zs == elem and elem == TILE and 4 * rows == TILE
    devices = slabs * planes
    parts, arrays = matrices(elem, rows, across)
    total = parts[-1][0] + parts[-1][1] + TILE
    vmem = pl.BlockSpec(memory_space=pltpu.VMEM)
    hbm = pl.BlockSpec(memory_space=pl.ANY)
    stages = ITERS + 1
    dma = pltpu.SemaphoreType.DMA

    def held(*shape):
        return pltpu.VMEM(shape, F32)

    return pl.pallas_call(
        functools.partial(kernel, slabs, planes, parts),
        out_shape=(
            jax.ShapeDtypeStruct(initial_displacement.shape, F32),
            jax.ShapeDtypeStruct(images.shape[1:], F32),
        ),
        in_specs=[hbm] + [vmem] * (2 + len(arrays)),
        out_specs=(vmem, hbm),
        scratch_shapes=[
            held(zs + 4, ys + 2 * TILE, xs),
            held(zs + 2, ys + 2 * TILE, xs),
            held(2, 3 * zs, xs),
            held(2, 3 * zs, xs),
            held(4, zs, xs),
            held(stages, TILE, across),
            held(stages, 9, TILE, across),
            held(stages, devices, 2, across),
            held(COMPS, zs, ys, xs),
            held(zs, ys, xs),
            held(4 * TILE, xs),
            held(3, TILE, xs),
            held(len(PAIRS) * 3 * ys, xs),
            held(COMPS * 2 * ys, xs),
            held(total, 2 * across),
            held(total, 2 * across),
            held(COMPS * 9 * TILE, 2 * across),
            held(9, TILE, across),
            held(9, TILE, across),
            dma((2,)),
            dma,
            dma((2, 2)),
            dma((2, 2)),
            dma((2,)),
            dma((2,)),
            dma((4,)),
            dma((4,)),
            dma((stages, 8)),
            dma((stages, 8)),
            dma((stages,)),
            dma((stages,)),
            dma((3,)),
            dma((3,)),
        ],
        compiler_params=pltpu.CompilerParams(
            collective_id=0, has_side_effects=True, vmem_limit_bytes=40 * 1024 * 1024
        ),
        name="gauss_newton_step",
    )(images, shifts, initial_displacement, *[jnp.asarray(a) for a in arrays])


def solution(mesh):
    in_specs = (
        P(None, "slab", "plane", None),
        P(None, "slab", "plane", None),
        P(None, "slab", "plane", None),
    )
    out_specs = (P(None, "slab", "plane", None), P("slab", "plane", None))
    run = functools.partial(body, mesh.shape["slab"], mesh.shape["plane"])
    return jax.shard_map(run, mesh=mesh, in_specs=in_specs, out_specs=out_specs, check_vma=False)
```

```python
import functools

import jax
import jax.numpy as jnp
import numpy as np
from jax import lax
from jax.experimental import pallas as pl
from jax.experimental.pallas import tpu as pltpu
from jax.sharding import PartitionSpec as P

ITERS = 6
reg_weight = 4.0

MESH = pl.DeviceIdType.MESH
F32 = jnp.float32
BF16 = jnp.bfloat16
TILE = 8
COMPS = 3
PAIRS = ((0, 0), (0, 1), (0, 2), (1, 1), (1, 2), (2, 2))
AROUND = tuple((dz, dy) for dz in (-1, 0, 1) for dy in (-1, 0, 1) if (dz, dy) != (0, 0))


def place_of(dz, dy):
    return (dz + 1) * 3 + dy + 1


def pair_of(i, j):
    return PAIRS.index((min(i, j), max(i, j)))


def matrices(elem, rows, across):
    w = np.arange(elem) / elem
    squares = ((1 - w) ** 2, w * (1 - w), w**2)
    count = elem * across
    hats = np.zeros((count, across))
    stencil = np.zeros((count, 2 * across))
    spread = np.zeros((across, count))
    for e in range(across):
        at = slice(e * elem, (e + 1) * elem)
        spread[e, at] = 1
        hats[at, e] = 1 - w
        stencil[at, e] += squares[0]
        if e + 1 < across:
            hats[at, e + 1] = w
            stencil[at, e + 1] += squares[2]
            stencil[at, across + e] = squares[1]

    height = rows * elem
    depth = len(PAIRS) * 3 * height

    def column(ij, cz, row):
        start = (ij * 3 + cz) * height + row * elem
        return slice(start, start + elem)

    last = rows - 1
    slab_rows = [(ij, cz, cy, r) for ij in range(6) for cz in (1, 2) for cy in range(3) for r in range(rows)]
    plane_rows = [(ij, cz, cy, last) for ij in range(6) for cz in (0, 1) for cy in (1, 2)]
    diag_rows = [(ij, cz, cy, last) for ij in range(6) for cz in (1, 2) for cy in (1, 2)]
    parts = []
    start = 0
    for listed in (slab_rows, plane_rows, diag_rows):
        used = -(-len(listed) // TILE) * TILE
        parts.append((start, used))
        start += used + TILE
    total = start
    send = np.zeros((total, depth))
    index = [{}, {}, {}]
    for part, listed in enumerate((slab_rows, plane_rows, diag_rows)):
        for n, key in enumerate(listed):
            ij, cz, cy, r = key
            send[parts[part][0] + n, column(ij, cz, r)] = squares[cy]
            index[part][key] = parts[part][0] + n

    own = np.zeros((COMPS * 9 * TILE + TILE, depth))
    came = np.zeros((COMPS * 9 * TILE + TILE, total))
    for i in range(COMPS):
        for dz in (-1, 0, 1):
            for dy in (-1, 0, 1):
                for j in range(COMPS):
                    for r in range(rows):
                        out = (i * 9 + place_of(dz, dy)) * TILE + j * rows + r
                        ij = pair_of(i, j)
                        layers = {0: ((0, 0), (-1, 2)), 1: ((0, 1),), -1: ((-1, 1),)}[dz]
                        lines = {0: ((r, 0), (r - 1, 2)), 1: ((r, 1),), -1: ((r - 1, 1),)}[dy]
                        for layer, cz in layers:
                            for line, cy in lines:
                                if layer == 0 and line >= 0:
                                    own[out, column(ij, cz, line)] = squares[cy]
                                elif layer < 0 and line >= 0:
                                    came[out, index[0][(ij, cz, cy, line)]] = 1
                                elif layer == 0:
                                    came[out, index[1][(ij, cz, cy, last)]] = 1
                                else:
                                    came[out, index[2][(ij, cz, cy, last)]] = 1

    loads = np.zeros((4 * TILE, COMPS * 2 * height))

    def line_of(i, cz, row):
        start = (i * 2 + cz) * height + row * elem
        return slice(start, start + elem)

    for i in range(COMPS):
        for r in range(rows):
            out = i * rows + r
            for cz in (0, 1):
                loads[cz * TILE + out, line_of(i, cz, r)] = 1 - w
                if r > 0:
                    loads[cz * TILE + out, line_of(i, cz, r - 1)] = w
        for cz in (0, 1):
            loads[(2 + cz) * TILE + i * rows, line_of(i, cz, last)] = w
    arrays = (stencil, hats, hats.T, spread, send, own, came, loads)
    return parts, [np.asarray(a, dtype=np.float32) for a in arrays]


def split(x):
    high = x.astype(BF16)
    return high, (x - high.astype(F32)).astype(BF16)


def dot(a, b):
    return jnp.dot(a, b, preferred_element_type=F32)


def dot_left(x, exact):
    high, low = split(x)
    return dot(high, exact) + dot(low, exact)


def dot_right(exact, x):
    high, low = split(x)
    return dot(exact, high) + dot(exact, low)


def kernel(
    slabs,
    planes,
    parts,
    images,
    shifts_in,
    start_in,
    w_stencil_in,
    w_hats_in,
    w_nodes_in,
    w_spread_in,
    w_send_in,
    w_own_in,
    w_came_in,
    w_loads_in,
    out_field,
    out_mismatch,
    ref_ext,
    def_ext,
    pack,
    got_rows,
    got_diag,
    tiles,
    halo,
    dots,
    grads,
    mis,
    nodes_x,
    moves,
    moments,
    loads,
    send_buf,
    got_buf,
    coefs,
    res,
    img,
    shifts,
    start_field,
    w_stencil,
    w_hats,
    w_nodes,
    w_spread,
    w_send,
    w_own,
    w_came,
    w_loads,
    load_sem,
    const_sem,
    out_sem,
    face_send,
    face_recv,
    row_send,
    row_recv,
    diag_send,
    diag_recv,
    tile_send,
    tile_recv,
    dot_send,
    dot_recv,
    part_send,
    part_recv,
):
    _, zs, ys, xs = images.shape
    rows, across = shifts_in.shape[2], shifts_in.shape[3]
    elem = xs // across
    devices = slabs * planes
    slab, plane = lax.axis_index("slab"), lax.axis_index("plane")
    me = slab * planes + plane

    def present(dz, dy):
        ok = None
        for d, at, count in ((dz, slab, slabs), (dy, plane, planes)):
            if d:
                here = at < count - 1 if d > 0 else at > 0
                ok = here if ok is None else jnp.logical_and(ok, here)
        return ok

    def beside(dz, dy):
        return (slab + dz, plane + dy)

    plane_to = [plane] + [jnp.where(plane + k < planes, plane + k, plane + k - planes) for k in range(1, planes)]

    def everyone(action):
        for to in plane_to[1:]:
            action((slab, to))

        def there(k, carry):
            at = jnp.where(slab + k < slabs, slab + k, slab + k - slabs)
            for to in plane_to:
                action((at, to))
            return carry

        lax.fori_loop(1, slabs, there, 0)

    mine = [
        pltpu.make_async_copy(images.at[0], ref_ext.at[pl.ds(2, zs), pl.ds(TILE, ys)], load_sem.at[0]),
        pltpu.make_async_copy(images.at[1], def_ext.at[pl.ds(1, zs), pl.ds(TILE, ys)], load_sem.at[1]),
    ]
    small = [
        pltpu.make_async_copy(src, dst, const_sem.at[n])
        for n, (src, dst) in enumerate(
            (
                (start_in, start_field),
                (shifts_in, shifts),
                (w_spread_in, w_spread),
                (w_nodes_in, w_nodes),
                (w_stencil_in, w_stencil),
                (w_hats_in, w_hats),
                (w_loads_in, w_loads),
                (w_send_in, w_send),
                (w_own_in, w_own),
                (w_came_in, w_came),
            )
        )
    ]
    for copy in mine + small:
        copy.start()
    halo[...] = jnp.zeros(halo.shape, F32)
    tiles[...] = jnp.zeros(tiles.shape, F32)
    got_buf[...] = jnp.zeros(got_buf.shape, F32)
    barrier = pltpu.get_barrier_semaphore()
    everyone(lambda to: pl.semaphore_signal(barrier, inc=1, device_id=to, device_id_type=MESH))
    for copy in small[:1] + mine:
        copy.wait()
    for j in range(COMPS):
        tiles[0, j * rows : (j + 1) * rows, :] = start_field[j, 0]

    for side, (far, near) in enumerate(((1, 0), (ys - 2, ys - 1))):
        pack[side, 0:zs, :] = ref_ext[2 : 2 + zs, TILE + far, :]
        pack[side, zs : 2 * zs, :] = ref_ext[2 : 2 + zs, TILE + near, :]
        pack[side, 2 * zs :, :] = def_ext[1 : 1 + zs, TILE + near, :]
    pl.semaphore_wait(barrier, devices - 1)

    def remote(src, dst, send, recv, to):
        return pltpu.make_async_remote_copy(
            src_ref=src, dst_ref=dst, send_sem=send, recv_sem=recv, device_id=to, device_id_type=MESH
        )

    def faces():
        out = []
        for n, d in enumerate((-1, 1)):
            low = 0 if d < 0 else zs - 2
            here = ref_ext.at[pl.ds(2 + low, 2), pl.ds(TILE, ys)]
            there = ref_ext.at[pl.ds(2 + zs if d < 0 else 0, 2), pl.ds(TILE, ys)]
            out.append(((d, 0), remote(here, there, face_send.at[n, 0], face_recv.at[n, 0], beside(d, 0))))
            low = 0 if d < 0 else zs - 1
            here = def_ext.at[pl.ds(1 + low, 1), pl.ds(TILE, ys)]
            there = def_ext.at[pl.ds(1 + zs if d < 0 else 0, 1), pl.ds(TILE, ys)]
            out.append(((d, 0), remote(here, there, face_send.at[n, 1], face_recv.at[n, 1], beside(d, 0))))
        for n, d in enumerate((-1, 1)):
            out.append(
                ((0, d), remote(pack.at[n], got_rows.at[n], row_send.at[n], row_recv.at[n], beside(0, d)))
            )
        for n, (dz, dy) in enumerate(((-1, -1), (-1, 1), (1, -1), (1, 1))):
            here = pack.at[(dy + 1) // 2, pl.ds(2 * zs, zs)]
            out.append(
                ((dz, dy), remote(here, got_diag.at[n], diag_send.at[n], diag_recv.at[n], beside(dz, dy)))
            )
        return out

    def around(stage):
        out = []
        for n, (dz, dy) in enumerate(AROUND):
            copy = remote(
                tiles.at[stage],
                halo.at[stage, place_of(-dz, -dy)],
                tile_send.at[stage, n],
                tile_recv.at[stage, n],
                beside(dz, dy),
            )
            out.append(((dz, dy), copy))
        return out

    def begin(copies):
        for (dz, dy), copy in copies:
            pl.when(present(dz, dy))(copy.start)

    def arrive(copies):
        for (dz, dy), copy in copies:
            pl.when(present(-dz, -dy))(copy.wait_recv)

    def sent(copies):
        for (dz, dy), copy in copies:
            pl.when(present(dz, dy))(copy.wait_send)

    def share(stage):
        slot = dots.at[stage, me]
        everyone(lambda to: remote(slot, slot, dot_send.at[stage], dot_recv.at[stage], to).start())

    def shared(sem, stage):
        some = dots.at[stage, pl.ds(0, devices - 1)]
        pltpu.make_async_copy(some, some, sem.at[stage]).wait()

    def totals(stage):
        shared(dot_recv, stage)
        lanes = jnp.sum(dots[stage], axis=0)
        return jnp.sum(lanes, axis=1, keepdims=True)

    image_copies = faces()
    start_copies = around(0)
    begin(image_copies[:4])
    begin(start_copies)
    begin(image_copies[4:])
    for copy in small[1:]:
        copy.wait()

    codes = jnp.concatenate([shifts[j, 0] for j in range(COMPS)], axis=0).astype(F32).astype(BF16)
    wide = dot(codes, w_spread[...].astype(BF16))
    for n, dx in enumerate((-1, 0, 1)):
        moves[n, 0 : COMPS * rows, :] = pltpu.roll(wide, dx % xs, 1) if dx else wide

    arrive(start_copies)
    halo[0, place_of(0, 0)] = tiles[0]
    corner = jnp.concatenate([halo[0, place_of(dz, dy)] for dz in (0, 1) for dy in (0, 1)], axis=0)
    nodes_x[...] = dot_left(corner, w_nodes[...].astype(BF16))

    arrive(image_copies[4:6])

    def clear(dz, dy, *views):
        def run():
            for ref, index in views:
                ref[index] = jnp.zeros(ref[index].shape, F32)

        pl.when(jnp.logical_not(present(dz, dy)))(run)

    for n, d in enumerate((1, -1)):
        clear(0, d, (got_rows, (n,)))
    top = TILE + ys
    ref_ext[2 : 2 + zs, top, :] = got_rows[0, zs : 2 * zs, :]
    ref_ext[2 : 2 + zs, top + 1, :] = got_rows[0, 0:zs, :]
    def_ext[1 : 1 + zs, top, :] = got_rows[0, 2 * zs :, :]
    ref_ext[2 : 2 + zs, TILE - 2, :] = got_rows[1, 0:zs, :]
    ref_ext[2 : 2 + zs, TILE - 1, :] = got_rows[1, zs : 2 * zs, :]
    def_ext[1 : 1 + zs, TILE - 1, :] = got_rows[1, 2 * zs :, :]
    lane = lax.broadcasted_iota(jnp.int32, (TILE, xs), 1)
    up = lax.broadcasted_iota(jnp.int32, (TILE, xs), 0).astype(F32) / elem

    def along(value, d):
        rolled = pltpu.roll(value, (-d) % xs, 1)
        inside = lane < xs - d if d > 0 else lane >= -d
        return jnp.where(inside, rolled, 0.0)

    def voxels(z, energy):
        wz = z.astype(F32) / elem
        for r in range(rows):
            base = TILE + r * elem

            def ref(dz, dy):
                return ref_ext[z + (2 + dz), base + dy : base + dy + elem, :]

            centre = ref(0, 0)
            g = [
                (ref(-2, 0) - ref(2, 0) + 8.0 * (ref(1, 0) - ref(-1, 0))) * (1.0 / 12.0),
                (ref(0, -2) - ref(0, 2) + 8.0 * (ref(0, 1) - ref(0, -1))) * (1.0 / 12.0),
                (
                    along(centre, -2)
                    - along(centre, 2)
                    + 8.0 * (along(centre, 1) - along(centre, -1))
                )
                * (1.0 / 12.0),
            ]
            warped = None
            for n, dx in enumerate((-1, 0, 1)):
                s = [moves[n, j * rows + r : j * rows + r + 1, :] for j in range(2)]
                s = [jnp.broadcast_to(v, (elem, xs)) for v in s]
                below, above = s[0] < -0.5, s[0] > 0.5
                line = []
                for dy in (-1, 0, 1):
                    at = pl.ds(base + dy, elem)
                    value = jnp.where(below, def_ext[z, at, :], def_ext[z + 1, at, :])
                    line.append(jnp.where(above, def_ext[z + 2, at, :], value))
                value = jnp.where(s[1] < -0.5, line[0], line[1])
                value = jnp.where(s[1] > 0.5, line[2], value)
                if dx:
                    value = along(value, dx)
                sx = jnp.broadcast_to(moves[1, 2 * rows + r : 2 * rows + r + 1, :], (elem, xs))
                if warped is None:
                    warped = value
                else:
                    warped = jnp.where(sx > dx - 0.5, value, warped)
            total = centre - warped
            for j in range(COMPS):

                def node(line):
                    dy = line // rows
                    at = j * rows + line % rows
                    low = nodes_x[dy * TILE + at : dy * TILE + at + 1, :]
                    high = nodes_x[(2 + dy) * TILE + at : (2 + dy) * TILE + at + 1, :]
                    return (1.0 - wz) * low + wz * high

                moved = (1.0 - up) * node(r) + up * node(r + 1)
                total = total - g[j] * moved
                grads[j, z, r * elem : (r + 1) * elem, :] = g[j]
                energy = energy + g[j] * g[j]
            mis[z, r * elem : (r + 1) * elem, :] = total
        return energy

    energy = lax.fori_loop(2, zs - 2, voxels, jnp.zeros((TILE, xs), F32))
    arrive(image_copies[:4] + image_copies[6:])
    clear(-1, 0, (ref_ext, (slice(0, 2),)), (def_ext, (slice(0, 1),)))
    clear(1, 0, (ref_ext, (slice(2 + zs, 4 + zs),)), (def_ext, (slice(1 + zs, 2 + zs),)))
    for n, (dz, dy) in enumerate(((1, 1), (1, -1), (-1, 1), (-1, -1))):
        clear(dz, dy, (got_diag, (n,)))
    def_ext[1 + zs, top : top + 1, :] = got_diag[0, 0:1, :]
    def_ext[1 + zs, TILE - 1 : TILE, :] = got_diag[1, 0:1, :]
    def_ext[0, top : top + 1, :] = got_diag[2, zs - 1 : zs, :]
    def_ext[0, TILE - 1 : TILE, :] = got_diag[3, zs - 1 : zs, :]
    energy = lax.fori_loop(0, 2, voxels, energy)
    energy = lax.fori_loop(zs - 2, zs, voxels, energy)
    store = pltpu.make_async_copy(mis, out_mismatch, out_sem)
    store.start()
    energy = jnp.sum(energy, axis=0, keepdims=True)
    dots[0, me] = jnp.zeros(dots.shape[2:], F32)
    row = energy[:, :across]
    for c in range(1, xs // across):
        row = row + energy[:, c * across : (c + 1) * across]
    dots[0, me, 0:1, :] = row
    share(0)

    width = 128
    lines = xs // width

    def gather(n, carry):
        r, c = lax.div(n, lines), lax.rem(n, lines)
        ay = pl.ds(pl.multiple_of(r * elem, elem), elem)
        ax = pl.ds(pl.multiple_of(c * width, width), width)
        sums = [[None] * 3 for _ in PAIRS]
        forces = [[None] * 2 for _ in range(COMPS)]

        def add(total, weight, value):
            if weight == 0.0:
                return total
            term = value if weight == 1.0 else weight * value
            return term if total is None else total + term

        for z in range(zs):
            w = z / elem
            g = [grads[j, z, ay, ax] for j in range(COMPS)]
            q = mis[z, ay, ax]
            for ij, (i, j) in enumerate(PAIRS):
                product = g[i] * g[j]
                for cz, weight in enumerate(((1 - w) ** 2, w * (1 - w), w * w)):
                    sums[ij][cz] = add(sums[ij][cz], weight, product)
            for i in range(COMPS):
                product = g[i] * q
                for cz, weight in enumerate((1 - w, w)):
                    forces[i][cz] = add(forces[i][cz], weight, product)
        for ij in range(len(PAIRS)):
            for cz in range(3):
                at = pl.multiple_of((ij * 3 + cz) * ys + r * elem, elem)
                moments[pl.ds(at, elem), ax] = sums[ij][cz]
        for i in range(COMPS):
            for cz in range(2):
                at = pl.multiple_of((i * 2 + cz) * ys + r * elem, elem)
                loads[pl.ds(at, elem), ax] = forces[i][cz]
        return carry

    lax.fori_loop(0, rows * lines, gather, 0)
    summed = dot_left(moments[...], w_stencil[...].astype(BF16))
    load_tiles = dot_right(w_loads[...].astype(BF16), dot_left(loads[...], w_hats[...].astype(BF16)))
    send_buf[...] = dot_right(w_send[...].astype(BF16), summed)
    for (start, used), n in zip(parts, (1, 2, 3)):
        send_buf[start + used : start + used + TILE, :across] = load_tiles[n * TILE : (n + 1) * TILE]
    part_copies = []
    for n, ((start, used), to) in enumerate(zip(parts, ((1, 0), (0, 1), (1, 1)))):
        at = pl.ds(start, used + TILE)
        part_copies.append(
            (to, remote(send_buf.at[at], got_buf.at[at], part_send.at[n], part_recv.at[n], beside(*to)))
        )
    begin(part_copies)
    coefs[...] = dot_right(w_own[...].astype(BF16), summed)

    node_lane = lax.broadcasted_iota(jnp.int32, (TILE, across), 1)
    sub = lax.broadcasted_iota(jnp.int32, (TILE, across), 0)
    line = lax.rem(sub, rows)
    group = lax.div(sub, rows)

    def neighbour(get, dz, dy):
        centre = get(place_of(dz, 0))
        if dy == 0:
            return centre
        edge = get(place_of(dz, dy))
        inner = pltpu.roll(centre, (-dy) % TILE, 0)
        outer = pltpu.roll(edge, (dy * (rows - 1)) % TILE, 0)
        return jnp.where(line == (rows - 1 if dy > 0 else 0), outer, inner)

    def start_at(place):
        return halo[0, place]

    centre = start_at(place_of(0, 0))
    lap = 6.0 * centre - neighbour(start_at, -1, 0) - neighbour(start_at, 1, 0)
    lap = lap - neighbour(start_at, 0, -1) - neighbour(start_at, 0, 1)
    lap = lap - jnp.where(node_lane > 0, pltpu.roll(centre, 1, 1), 0.0)
    lap = lap - jnp.where(node_lane < across - 1, pltpu.roll(centre, across - 1, 1), 0.0)
    lap = jnp.where(group < COMPS, lap, 0.0)

    penalty = totals(0)[0:1, :] * (reg_weight / (devices * zs * ys * xs))
    arrive(part_copies)
    rhs = load_tiles[0:TILE] - penalty * lap
    for start, used in parts:
        rhs = rhs + got_buf[start + used : start + used + TILE, :across]
    tiles[1] = rhs
    rhs_copies = around(1)
    begin(rhs_copies)

    coefs[...] = coefs[...] + dot_right(w_came[...].astype(BF16), got_buf[...])
    for i in range(COMPS):
        same = jnp.where(group == i, 1.0, 0.0) * penalty

        def raise_by(dz, dy, part, value):
            at = pl.ds((i * 9 + place_of(dz, dy)) * TILE, TILE)
            to = pl.ds(part * across, across)
            coefs[at, to] = coefs[at, to] + value

        raise_by(0, 0, 0, 6.0 * same)
        raise_by(0, 0, 1, jnp.where(node_lane < across - 1, -same, 0.0))
        for dz, dy in ((-1, 0), (1, 0), (0, -1), (0, 1)):
            raise_by(dz, dy, 0, -same)

    arrive(rhs_copies)
    halo[1, place_of(0, 0)] = rhs
    res[...] = halo[1]
    img[...] = jnp.zeros(img.shape, F32)

    def operate():
        out = [None] * COMPS
        back = [None] * COMPS
        for dz in (-1, 0, 1):
            for dy in (-1, 0, 1):
                v = neighbour(lambda place: res[place], dz, dy)
                ahead = pltpu.roll(v, across - 1, 1)
                for i in range(COMPS):
                    at = pl.ds((i * 9 + place_of(dz, dy)) * TILE, TILE)
                    here, link = coefs[at, 0:across], coefs[at, across : 2 * across]
                    term = here * v + link * ahead
                    out[i] = term if out[i] is None else out[i] + term
                    term = link * v
                    back[i] = term if back[i] is None else back[i] + term
        image = jnp.zeros((TILE, across), F32)
        for i in range(COMPS):
            value = out[i] + pltpu.roll(back[i], 1, 1)
            value = value + pltpu.roll(value, TILE // 2, 0)
            value = value + pltpu.roll(value, rows, 0)
            image = jnp.where(group == i, value, image)
        return image

    direction = jnp.zeros((TILE, across), F32)
    step = jnp.zeros((TILE, across), F32)
    norm_before = size_before = None
    copies = [image_copies, start_copies, part_copies, rhs_copies]
    for k in range(ITERS):
        image = operate()
        residual = res[place_of(0, 0)]
        stage = k + 1
        dots[stage, me, 0:1, :] = jnp.sum(residual * residual, axis=0, keepdims=True)
        dots[stage, me, 1:2, :] = jnp.sum(residual * image, axis=0, keepdims=True)
        share(stage)
        if k < ITERS - 1:
            tiles[stage + 1] = image
            halo_copies = around(stage + 1)
            begin(halo_copies)
            copies.append(halo_copies)
        sums = totals(stage)
        norm, inner = sums[0:1, :], sums[1:2, :]
        if k == 0:
            size = norm / inner
            direction = residual
        else:
            ratio = norm / norm_before
            size = norm / (inner - ratio * norm / size_before)
            direction = residual + ratio * direction
        step = step + size * direction
        norm_before, size_before = norm, size
        if k < ITERS - 1:
            arrive(halo_copies)
            halo[stage + 1, place_of(0, 0)] = image
            flow = halo[stage + 1]
            if k > 0:
                flow = flow + ratio * img[...]
            img[...] = flow
            res[...] = res[...] - size * flow

    result = tiles[0] + step
    for j in range(COMPS):
        out_field[j, 0] = result[j * rows : (j + 1) * rows]
    for listed in copies:
        sent(listed)
    for stage in range(ITERS + 1):
        shared(dot_send, stage)
    store.wait()


def body(slabs, planes, images, shifts, initial_displacement):
    _, zs, ys, xs = images.shape
    layers, rows, across = shifts.shape[1:]
    elem = xs // across
    assert layers == 1 and zs == elem and elem == TILE and 4 * rows == TILE
    devices = slabs * planes
    parts, arrays = matrices(elem, rows, across)
    total = parts[-1][0] + parts[-1][1] + TILE
    vmem = pl.BlockSpec(memory_space=pltpu.VMEM)
    hbm = pl.BlockSpec(memory_space=pltpu.HBM)
    stages = ITERS + 1
    dma = pltpu.SemaphoreType.DMA

    def held(*shape):
        return pltpu.VMEM(shape, F32)

    return pl.pallas_call(
        functools.partial(kernel, slabs, planes, parts),
        out_shape=(
            jax.ShapeDtypeStruct(initial_displacement.shape, F32),
            jax.ShapeDtypeStruct(images.shape[1:], F32),
        ),
        in_specs=[hbm] * (3 + len(arrays)),
        out_specs=(vmem, hbm),
        scratch_shapes=[
            held(zs + 4, ys + 2 * TILE, xs),
            held(zs + 2, ys + 2 * TILE, xs),
            held(2, 3 * zs, xs),
            held(2, 3 * zs, xs),
            held(4, zs, xs),
            held(stages, TILE, across),
            held(stages, 9, TILE, across),
            held(stages, devices, 2, across),
            held(COMPS, zs, ys, xs),
            held(zs, ys, xs),
            held(4 * TILE, xs),
            held(3, TILE, xs),
            held(len(PAIRS) * 3 * ys, xs),
            held(COMPS * 2 * ys, xs),
            held(total, 2 * across),
            held(total, 2 * across),
            held(COMPS * 9 * TILE + TILE, 2 * across),
            held(9, TILE, across),
            held(9, TILE, across),
            pltpu.VMEM(shifts.shape, jnp.int32),
            held(*initial_displacement.shape),
            *[held(*a.shape) for a in arrays],
            dma((2,)),
            dma((2 + len(arrays),)),
            dma,
            dma((2, 2)),
            dma((2, 2)),
            dma((2,)),
            dma((2,)),
            dma((4,)),
            dma((4,)),
            dma((stages, 8)),
            dma((stages, 8)),
            dma((stages,)),
            dma((stages,)),
            dma((3,)),
            dma((3,)),
        ],
        compiler_params=pltpu.CompilerParams(
            collective_id=0, has_side_effects=True, vmem_limit_bytes=56 * 1024 * 1024
        ),
        name="gauss_newton_step",
    )(images, shifts, initial_displacement, *[jnp.asarray(a) for a in arrays])


def solution(mesh):
    in_specs = (
        P(None, "slab", "plane", None),
        P(None, "slab", "plane", None),
        P(None, "slab", "plane", None),
    )
    out_specs = (P(None, "slab", "plane", None), P("slab", "plane", None))
    run = functools.partial(body, mesh.shape["slab"], mesh.shape["plane"])
    return jax.shard_map(run, mesh=mesh, in_specs=in_specs, out_specs=out_specs, check_vma=False)
```

```python
import functools

import jax
import jax.numpy as jnp
import numpy as np
from jax import lax
from jax.experimental import pallas as pl
from jax.experimental.pallas import tpu as pltpu
from jax.sharding import PartitionSpec as P

ITERS = 6
BLOCK = ITERS // 2
SPREAD = 128.0
reg_weight = 4.0

MESH = pl.DeviceIdType.MESH
F32 = jnp.float32
BF16 = jnp.bfloat16
TILE = 8
COMPS = 3
PAIRS = ((0, 0), (0, 1), (0, 2), (1, 1), (1, 2), (2, 2))
AROUND = tuple((dz, dy) for dz in (-1, 0, 1) for dy in (-1, 0, 1) if (dz, dy) != (0, 0))


def place_of(dz, dy):
    return (dz + 1) * 3 + dy + 1


def pair_of(i, j):
    return PAIRS.index((min(i, j), max(i, j)))


def matrices(elem, rows, across):
    w = np.arange(elem) / elem
    squares = ((1 - w) ** 2, w * (1 - w), w**2)
    count = elem * across
    hats = np.zeros((count, across))
    stencil = np.zeros((count, 2 * across))
    spread = np.zeros((across, count))
    for e in range(across):
        at = slice(e * elem, (e + 1) * elem)
        spread[e, at] = 1
        hats[at, e] = 1 - w
        stencil[at, e] += squares[0]
        if e + 1 < across:
            hats[at, e + 1] = w
            stencil[at, e + 1] += squares[2]
            stencil[at, across + e] = squares[1]

    height = rows * elem
    depth = len(PAIRS) * 3 * height

    def column(ij, cz, row):
        start = (ij * 3 + cz) * height + row * elem
        return slice(start, start + elem)

    last = rows - 1
    slab_rows = [(ij, cz, cy, r) for ij in range(6) for cz in (1, 2) for cy in range(3) for r in range(rows)]
    plane_rows = [(ij, cz, cy, last) for ij in range(6) for cz in (0, 1) for cy in (1, 2)]
    diag_rows = [(ij, cz, cy, last) for ij in range(6) for cz in (1, 2) for cy in (1, 2)]
    parts = []
    start = 0
    for listed in (slab_rows, plane_rows, diag_rows):
        used = -(-len(listed) // TILE) * TILE
        parts.append((start, used))
        start += used + TILE
    total = start
    send = np.zeros((total, depth))
    index = [{}, {}, {}]
    for part, listed in enumerate((slab_rows, plane_rows, diag_rows)):
        for n, key in enumerate(listed):
            ij, cz, cy, r = key
            send[parts[part][0] + n, column(ij, cz, r)] = squares[cy]
            index[part][key] = parts[part][0] + n

    own = np.zeros((COMPS * 9 * TILE + TILE, depth))
    came = np.zeros((COMPS * 9 * TILE + TILE, total))
    for i in range(COMPS):
        for dz in (-1, 0, 1):
            for dy in (-1, 0, 1):
                for j in range(COMPS):
                    for r in range(rows):
                        out = (i * 9 + place_of(dz, dy)) * TILE + j * rows + r
                        ij = pair_of(i, j)
                        layers = {0: ((0, 0), (-1, 2)), 1: ((0, 1),), -1: ((-1, 1),)}[dz]
                        lines = {0: ((r, 0), (r - 1, 2)), 1: ((r, 1),), -1: ((r - 1, 1),)}[dy]
                        for layer, cz in layers:
                            for line, cy in lines:
                                if layer == 0 and line >= 0:
                                    own[out, column(ij, cz, line)] = squares[cy]
                                elif layer < 0 and line >= 0:
                                    came[out, index[0][(ij, cz, cy, line)]] = 1
                                elif layer == 0:
                                    came[out, index[1][(ij, cz, cy, last)]] = 1
                                else:
                                    came[out, index[2][(ij, cz, cy, last)]] = 1

    loads = np.zeros((4 * TILE, COMPS * 2 * height))

    def line_of(i, cz, row):
        start = (i * 2 + cz) * height + row * elem
        return slice(start, start + elem)

    for i in range(COMPS):
        for r in range(rows):
            out = i * rows + r
            for cz in (0, 1):
                loads[cz * TILE + out, line_of(i, cz, r)] = 1 - w
                if r > 0:
                    loads[cz * TILE + out, line_of(i, cz, r - 1)] = w
        for cz in (0, 1):
            loads[(2 + cz) * TILE + i * rows, line_of(i, cz, last)] = w
    arrays = (stencil, hats, hats.T, spread, send, own, came, loads)
    return parts, [np.asarray(a, dtype=np.float32) for a in arrays]


def split(x):
    high = x.astype(BF16)
    return high, (x - high.astype(F32)).astype(BF16)


def dot(a, b):
    return jnp.dot(a, b, preferred_element_type=F32)


def dot_left(x, exact):
    high, low = split(x)
    return dot(high, exact) + dot(low, exact)


def dot_right(exact, x):
    high, low = split(x)
    return dot(exact, high) + dot(exact, low)


def times(a, b):
    if isinstance(a, float) and a == 0.0 or isinstance(b, float) and b == 0.0:
        return 0.0
    if isinstance(a, float) and a == 1.0:
        return b
    if isinstance(b, float) and b == 1.0:
        return a
    return a * b


def total(a, b):
    if isinstance(a, float) and a == 0.0:
        return b
    if isinstance(b, float) and b == 0.0:
        return a
    return a + b


def lifted(poly):
    return [0.0] + list(poly)


def plus(a, b, factor):
    out = list(a) + [0.0] * (len(b) - len(a))
    for k, value in enumerate(b):
        out[k] = total(out[k], times(factor, value))
    return out


def product(a, b):
    out = [0.0] * (len(a) + len(b) - 1)
    for i, x in enumerate(a):
        for j, y in enumerate(b):
            out[i + j] = total(out[i + j], times(x, y))
    return out


def combine(poly, values):
    out = 0.0
    for k, value in enumerate(poly):
        if not (isinstance(value, float) and value == 0.0):
            out = total(out, times(value, values[k]))
    return out


def inner(x, y, moments):
    out = combine(product(x[0], y[0]), moments[0])
    mixed = plus(product(x[0], y[1]), product(x[1], y[0]), 1.0)
    out = total(out, combine(mixed, moments[1]))
    return total(out, combine(product(x[1], y[1]), moments[2]))


def conjugate(residual, direction, moments, shift, steps, go_on):
    moved = ([0.0], [0.0])
    norm = inner(residual, residual, moments)
    turns = 0.0
    past = None
    for k in range(steps):
        image = tuple(plus(lifted(d), d, shift) for d in direction)
        bend = inner(direction, image, moments)
        size = norm / bend
        moved = tuple(plus(m, d, size) for m, d in zip(moved, direction))
        if k == steps - 1 and not go_on:
            break
        before, old = residual, direction
        residual = tuple(plus(r, i, -size) for r, i in zip(residual, image))
        fresh = inner(residual, residual, moments)
        ratio = fresh / norm
        direction = tuple(plus(r, d, ratio) for r, d in zip(residual, direction))
        turns = total(turns, (bend / norm) * (1.0 / steps))
        norm = fresh
        past = (old[1], before[1], size, ratio, turns)
    return moved, residual, direction, past


def kernel(
    slabs,
    planes,
    parts,
    images,
    shifts_in,
    start_in,
    w_stencil_in,
    w_hats_in,
    w_nodes_in,
    w_spread_in,
    w_send_in,
    w_own_in,
    w_came_in,
    w_loads_in,
    out_field,
    out_mismatch,
    ref_ext,
    def_ext,
    pack,
    got_rows,
    got_diag,
    tiles,
    halo,
    dots,
    grads,
    mis,
    nodes_x,
    moves,
    moments,
    loads,
    send_buf,
    got_buf,
    coefs,
    res,
    shifts,
    start_field,
    w_stencil,
    w_hats,
    w_nodes,
    w_spread,
    w_send,
    w_own,
    w_came,
    w_loads,
    load_sem,
    const_sem,
    out_sem,
    face_send,
    face_recv,
    row_send,
    row_recv,
    diag_send,
    diag_recv,
    tile_send,
    tile_recv,
    dot_send,
    dot_recv,
    part_send,
    part_recv,
):
    _, zs, ys, xs = images.shape
    rows, across = shifts_in.shape[2], shifts_in.shape[3]
    elem = xs // across
    devices = slabs * planes
    slab, plane = lax.axis_index("slab"), lax.axis_index("plane")
    me = slab * planes + plane

    def present(dz, dy):
        ok = None
        for d, at, count in ((dz, slab, slabs), (dy, plane, planes)):
            if d:
                here = at < count - 1 if d > 0 else at > 0
                ok = here if ok is None else jnp.logical_and(ok, here)
        return ok

    def beside(dz, dy):
        return (slab + dz, plane + dy)

    plane_to = [plane] + [jnp.where(plane + k < planes, plane + k, plane + k - planes) for k in range(1, planes)]

    def everyone(action):
        for to in plane_to[1:]:
            action((slab, to))

        def there(k, carry):
            at = jnp.where(slab + k < slabs, slab + k, slab + k - slabs)
            for to in plane_to:
                action((at, to))
            return carry

        lax.fori_loop(1, slabs, there, 0)

    mine = [
        pltpu.make_async_copy(images.at[0], ref_ext.at[pl.ds(2, zs), pl.ds(TILE, ys)], load_sem.at[0]),
        pltpu.make_async_copy(images.at[1], def_ext.at[pl.ds(1, zs), pl.ds(TILE, ys)], load_sem.at[1]),
    ]
    small = [
        pltpu.make_async_copy(src, dst, const_sem.at[n])
        for n, (src, dst) in enumerate(
            (
                (start_in, start_field),
                (shifts_in, shifts),
                (w_spread_in, w_spread),
                (w_nodes_in, w_nodes),
                (w_stencil_in, w_stencil),
                (w_hats_in, w_hats),
                (w_loads_in, w_loads),
                (w_send_in, w_send),
                (w_own_in, w_own),
                (w_came_in, w_came),
            )
        )
    ]
    for copy in mine + small:
        copy.start()
    halo[...] = jnp.zeros(halo.shape, F32)
    tiles[...] = jnp.zeros(tiles.shape, F32)
    got_buf[...] = jnp.zeros(got_buf.shape, F32)
    barrier = pltpu.get_barrier_semaphore()
    everyone(lambda to: pl.semaphore_signal(barrier, inc=1, device_id=to, device_id_type=MESH))
    for copy in small[:1] + mine:
        copy.wait()
    for j in range(COMPS):
        tiles[0, j * rows : (j + 1) * rows, :] = start_field[j, 0]

    for side, (far, near) in enumerate(((1, 0), (ys - 2, ys - 1))):
        pack[side, 0:zs, :] = ref_ext[2 : 2 + zs, TILE + far, :]
        pack[side, zs : 2 * zs, :] = ref_ext[2 : 2 + zs, TILE + near, :]
        pack[side, 2 * zs :, :] = def_ext[1 : 1 + zs, TILE + near, :]
    pl.semaphore_wait(barrier, devices - 1)

    def remote(src, dst, send, recv, to):
        return pltpu.make_async_remote_copy(
            src_ref=src, dst_ref=dst, send_sem=send, recv_sem=recv, device_id=to, device_id_type=MESH
        )

    def faces():
        out = []
        for n, d in enumerate((-1, 1)):
            low = 0 if d < 0 else zs - 2
            here = ref_ext.at[pl.ds(2 + low, 2), pl.ds(TILE, ys)]
            there = ref_ext.at[pl.ds(2 + zs if d < 0 else 0, 2), pl.ds(TILE, ys)]
            out.append(((d, 0), remote(here, there, face_send.at[n, 0], face_recv.at[n, 0], beside(d, 0))))
            low = 0 if d < 0 else zs - 1
            here = def_ext.at[pl.ds(1 + low, 1), pl.ds(TILE, ys)]
            there = def_ext.at[pl.ds(1 + zs if d < 0 else 0, 1), pl.ds(TILE, ys)]
            out.append(((d, 0), remote(here, there, face_send.at[n, 1], face_recv.at[n, 1], beside(d, 0))))
        for n, d in enumerate((-1, 1)):
            out.append(
                ((0, d), remote(pack.at[n], got_rows.at[n], row_send.at[n], row_recv.at[n], beside(0, d)))
            )
        for n, (dz, dy) in enumerate(((-1, -1), (-1, 1), (1, -1), (1, 1))):
            here = pack.at[(dy + 1) // 2, pl.ds(2 * zs, zs)]
            out.append(
                ((dz, dy), remote(here, got_diag.at[n], diag_send.at[n], diag_recv.at[n], beside(dz, dy)))
            )
        return out

    def around(stage):
        out = []
        for n, (dz, dy) in enumerate(AROUND):
            copy = remote(
                tiles.at[stage],
                halo.at[stage, place_of(-dz, -dy)],
                tile_send.at[stage, n],
                tile_recv.at[stage, n],
                beside(dz, dy),
            )
            out.append(((dz, dy), copy))
        return out

    def begin(copies):
        for (dz, dy), copy in copies:
            pl.when(present(dz, dy))(copy.start)

    def arrive(copies):
        for (dz, dy), copy in copies:
            pl.when(present(-dz, -dy))(copy.wait_recv)

    def sent(copies):
        for (dz, dy), copy in copies:
            pl.when(present(dz, dy))(copy.wait_send)

    def share(stage):
        slot = dots.at[stage, me]
        everyone(lambda to: remote(slot, slot, dot_send.at[stage], dot_recv.at[stage], to).start())

    def shared(sem, stage):
        some = dots.at[stage, pl.ds(0, devices - 1)]
        pltpu.make_async_copy(some, some, sem.at[stage]).wait()

    def totals(stage):
        shared(dot_recv, stage)
        lanes = jnp.sum(dots[stage], axis=0)
        return jnp.sum(lanes, axis=1, keepdims=True)

    image_copies = faces()
    start_copies = around(0)
    begin(image_copies[:4])
    begin(start_copies)
    begin(image_copies[4:])
    for copy in small[1:]:
        copy.wait()

    codes = jnp.concatenate([shifts[j, 0] for j in range(COMPS)], axis=0).astype(F32).astype(BF16)
    wide = dot(codes, w_spread[...].astype(BF16))
    for n, dx in enumerate((-1, 0, 1)):
        moves[n, 0 : COMPS * rows, :] = pltpu.roll(wide, dx % xs, 1) if dx else wide

    arrive(start_copies)
    halo[0, place_of(0, 0)] = tiles[0]
    corner = jnp.concatenate([halo[0, place_of(dz, dy)] for dz in (0, 1) for dy in (0, 1)], axis=0)
    nodes_x[...] = dot_left(corner, w_nodes[...].astype(BF16))

    arrive(image_copies[4:6])

    def clear(dz, dy, *views):
        def run():
            for ref, index in views:
                ref[index] = jnp.zeros(ref[index].shape, F32)

        pl.when(jnp.logical_not(present(dz, dy)))(run)

    for n, d in enumerate((1, -1)):
        clear(0, d, (got_rows, (n,)))
    top = TILE + ys
    ref_ext[2 : 2 + zs, top, :] = got_rows[0, zs : 2 * zs, :]
    ref_ext[2 : 2 + zs, top + 1, :] = got_rows[0, 0:zs, :]
    def_ext[1 : 1 + zs, top, :] = got_rows[0, 2 * zs :, :]
    ref_ext[2 : 2 + zs, TILE - 2, :] = got_rows[1, 0:zs, :]
    ref_ext[2 : 2 + zs, TILE - 1, :] = got_rows[1, zs : 2 * zs, :]
    def_ext[1 : 1 + zs, TILE - 1, :] = got_rows[1, 2 * zs :, :]
    lane = lax.broadcasted_iota(jnp.int32, (TILE, xs), 1)
    up = lax.broadcasted_iota(jnp.int32, (TILE, xs), 0).astype(F32) / elem

    def along(value, d):
        rolled = pltpu.roll(value, (-d) % xs, 1)
        inside = lane < xs - d if d > 0 else lane >= -d
        return jnp.where(inside, rolled, 0.0)

    def voxels(z, energy):
        wz = z.astype(F32) / elem
        for r in range(rows):
            base = TILE + r * elem

            def ref(dz, dy):
                return ref_ext[z + (2 + dz), base + dy : base + dy + elem, :]

            centre = ref(0, 0)
            g = [
                (ref(-2, 0) - ref(2, 0) + 8.0 * (ref(1, 0) - ref(-1, 0))) * (1.0 / 12.0),
                (ref(0, -2) - ref(0, 2) + 8.0 * (ref(0, 1) - ref(0, -1))) * (1.0 / 12.0),
                (
                    along(centre, -2)
                    - along(centre, 2)
                    + 8.0 * (along(centre, 1) - along(centre, -1))
                )
                * (1.0 / 12.0),
            ]
            warped = None
            for n, dx in enumerate((-1, 0, 1)):
                s = [moves[n, j * rows + r : j * rows + r + 1, :] for j in range(2)]
                s = [jnp.broadcast_to(v, (elem, xs)) for v in s]
                below, above = s[0] < -0.5, s[0] > 0.5
                line = []
                for dy in (-1, 0, 1):
                    at = pl.ds(base + dy, elem)
                    value = jnp.where(below, def_ext[z, at, :], def_ext[z + 1, at, :])
                    line.append(jnp.where(above, def_ext[z + 2, at, :], value))
                value = jnp.where(s[1] < -0.5, line[0], line[1])
                value = jnp.where(s[1] > 0.5, line[2], value)
                if dx:
                    value = along(value, dx)
                sx = jnp.broadcast_to(moves[1, 2 * rows + r : 2 * rows + r + 1, :], (elem, xs))
                if warped is None:
                    warped = value
                else:
                    warped = jnp.where(sx > dx - 0.5, value, warped)
            total = centre - warped
            for j in range(COMPS):

                def node(line):
                    dy = line // rows
                    at = j * rows + line % rows
                    low = nodes_x[dy * TILE + at : dy * TILE + at + 1, :]
                    high = nodes_x[(2 + dy) * TILE + at : (2 + dy) * TILE + at + 1, :]
                    return (1.0 - wz) * low + wz * high

                moved = (1.0 - up) * node(r) + up * node(r + 1)
                total = total - g[j] * moved
                grads[j, z, r * elem : (r + 1) * elem, :] = g[j]
                energy = energy + g[j] * g[j]
            mis[z, r * elem : (r + 1) * elem, :] = total
        return energy

    energy = lax.fori_loop(2, zs - 2, voxels, jnp.zeros((TILE, xs), F32))
    arrive(image_copies[:4] + image_copies[6:])
    clear(-1, 0, (ref_ext, (slice(0, 2),)), (def_ext, (slice(0, 1),)))
    clear(1, 0, (ref_ext, (slice(2 + zs, 4 + zs),)), (def_ext, (slice(1 + zs, 2 + zs),)))
    for n, (dz, dy) in enumerate(((1, 1), (1, -1), (-1, 1), (-1, -1))):
        clear(dz, dy, (got_diag, (n,)))
    def_ext[1 + zs, top : top + 1, :] = got_diag[0, 0:1, :]
    def_ext[1 + zs, TILE - 1 : TILE, :] = got_diag[1, 0:1, :]
    def_ext[0, top : top + 1, :] = got_diag[2, zs - 1 : zs, :]
    def_ext[0, TILE - 1 : TILE, :] = got_diag[3, zs - 1 : zs, :]
    energy = lax.fori_loop(0, 2, voxels, energy)
    energy = lax.fori_loop(zs - 2, zs, voxels, energy)
    store = pltpu.make_async_copy(mis, out_mismatch, out_sem)
    store.start()
    energy = jnp.sum(energy, axis=0, keepdims=True)
    dots[0, me] = jnp.zeros(dots.shape[2:], F32)
    row = energy[:, :across]
    for c in range(1, xs // across):
        row = row + energy[:, c * across : (c + 1) * across]
    dots[0, me, 0:1, :] = row
    share(0)

    width = 128
    lines = xs // width

    def gather(n, carry):
        r, c = lax.div(n, lines), lax.rem(n, lines)
        ay = pl.ds(pl.multiple_of(r * elem, elem), elem)
        ax = pl.ds(pl.multiple_of(c * width, width), width)
        sums = [[None] * 3 for _ in PAIRS]
        forces = [[None] * 2 for _ in range(COMPS)]

        def add(total, weight, value):
            if weight == 0.0:
                return total
            term = value if weight == 1.0 else weight * value
            return term if total is None else total + term

        for z in range(zs):
            w = z / elem
            g = [grads[j, z, ay, ax] for j in range(COMPS)]
            q = mis[z, ay, ax]
            for ij, (i, j) in enumerate(PAIRS):
                product = g[i] * g[j]
                for cz, weight in enumerate(((1 - w) ** 2, w * (1 - w), w * w)):
                    sums[ij][cz] = add(sums[ij][cz], weight, product)
            for i in range(COMPS):
                product = g[i] * q
                for cz, weight in enumerate((1 - w, w)):
                    forces[i][cz] = add(forces[i][cz], weight, product)
        for ij in range(len(PAIRS)):
            for cz in range(3):
                at = pl.multiple_of((ij * 3 + cz) * ys + r * elem, elem)
                moments[pl.ds(at, elem), ax] = sums[ij][cz]
        for i in range(COMPS):
            for cz in range(2):
                at = pl.multiple_of((i * 2 + cz) * ys + r * elem, elem)
                loads[pl.ds(at, elem), ax] = forces[i][cz]
        return carry

    lax.fori_loop(0, rows * lines, gather, 0)
    summed = dot_left(moments[...], w_stencil[...].astype(BF16))
    load_tiles = dot_right(w_loads[...].astype(BF16), dot_left(loads[...], w_hats[...].astype(BF16)))
    send_buf[...] = dot_right(w_send[...].astype(BF16), summed)
    for (start, used), n in zip(parts, (1, 2, 3)):
        send_buf[start + used : start + used + TILE, :across] = load_tiles[n * TILE : (n + 1) * TILE]
    part_copies = []
    for n, ((start, used), to) in enumerate(zip(parts, ((1, 0), (0, 1), (1, 1)))):
        at = pl.ds(start, used + TILE)
        part_copies.append(
            (to, remote(send_buf.at[at], got_buf.at[at], part_send.at[n], part_recv.at[n], beside(*to)))
        )
    begin(part_copies)
    coefs[...] = dot_right(w_own[...].astype(BF16), summed)

    node_lane = lax.broadcasted_iota(jnp.int32, (TILE, across), 1)
    sub = lax.broadcasted_iota(jnp.int32, (TILE, across), 0)
    line = lax.rem(sub, rows)
    group = lax.div(sub, rows)

    def neighbour(get, dz, dy):
        centre = get(place_of(dz, 0))
        if dy == 0:
            return centre
        edge = get(place_of(dz, dy))
        inner = pltpu.roll(centre, (-dy) % TILE, 0)
        outer = pltpu.roll(edge, (dy * (rows - 1)) % TILE, 0)
        return jnp.where(line == (rows - 1 if dy > 0 else 0), outer, inner)

    def start_at(place):
        return halo[0, place]

    centre = start_at(place_of(0, 0))
    lap = 6.0 * centre - neighbour(start_at, -1, 0) - neighbour(start_at, 1, 0)
    lap = lap - neighbour(start_at, 0, -1) - neighbour(start_at, 0, 1)
    lap = lap - jnp.where(node_lane > 0, pltpu.roll(centre, 1, 1), 0.0)
    lap = lap - jnp.where(node_lane < across - 1, pltpu.roll(centre, across - 1, 1), 0.0)
    lap = jnp.where(group < COMPS, lap, 0.0)

    penalty = totals(0)[0:1, :] * (reg_weight / (devices * zs * ys * xs))
    arrive(part_copies)
    rhs = load_tiles[0:TILE] - penalty * lap
    for start, used in parts:
        rhs = rhs + got_buf[start + used : start + used + TILE, :across]
    tiles[1] = rhs
    rhs_copies = around(1)
    begin(rhs_copies)

    coefs[...] = coefs[...] + dot_right(w_came[...].astype(BF16), got_buf[...])
    for i in range(COMPS):
        same = jnp.where(group == i, 1.0, 0.0) * penalty

        def raise_by(dz, dy, part, value):
            at = pl.ds((i * 9 + place_of(dz, dy)) * TILE, TILE)
            to = pl.ds(part * across, across)
            coefs[at, to] = coefs[at, to] + value

        raise_by(0, 0, 0, 6.0 * same)
        raise_by(0, 0, 1, jnp.where(node_lane < across - 1, -same, 0.0))
        for dz, dy in ((-1, 0), (1, 0), (0, -1), (0, 1)):
            raise_by(dz, dy, 0, -same)

    arrive(rhs_copies)
    halo[1, place_of(0, 0)] = rhs
    scale = 1.0 / (penalty * SPREAD)

    def operate(get, shift):
        out = [None] * COMPS
        back = [None] * COMPS
        for dz in (-1, 0, 1):
            for dy in (-1, 0, 1):
                v = neighbour(get, dz, dy)
                ahead = pltpu.roll(v, across - 1, 1)
                for i in range(COMPS):
                    at = pl.ds((i * 9 + place_of(dz, dy)) * TILE, TILE)
                    here, link = coefs[at, 0:across], coefs[at, across : 2 * across]
                    term = here * v + link * ahead
                    out[i] = term if out[i] is None else out[i] + term
                    term = link * v
                    back[i] = term if back[i] is None else back[i] + term
        image = jnp.zeros((TILE, across), F32)
        for i in range(COMPS):
            value = out[i] + pltpu.roll(back[i], 1, 1)
            value = value + pltpu.roll(value, TILE // 2, 0)
            value = value + pltpu.roll(value, rows, 0)
            image = jnp.where(group == i, value, image)
        return image * scale - shift * get(place_of(0, 0))

    copies = [image_copies, start_copies, part_copies, rhs_copies]

    def spread(stage, image):
        tiles[stage] = image
        listed = around(stage)
        begin(listed)
        copies.append(listed)
        return listed

    def landed(stage, listed, image):
        arrive(listed)
        halo[stage, place_of(0, 0)] = image

    def publish(stage, products):
        lines = [jnp.sum(p, axis=0, keepdims=True) for p in products]
        fill = -len(lines) % TILE
        lines += [jnp.zeros((1, across), F32)] * fill
        stacked = jnp.concatenate(lines, axis=0)
        column = jnp.sum(stacked, axis=1, keepdims=True)
        at = lax.broadcasted_iota(jnp.int32, stacked.shape, 0) == lax.broadcasted_iota(jnp.int32, stacked.shape, 1)
        dots[stage, me] = jnp.zeros(dots.shape[2:], F32)
        dots[stage, me, 0:1, :] = jnp.sum(jnp.where(at, column, 0.0), axis=0, keepdims=True)
        share(stage)

    def gathered(stage, count):
        shared(dot_recv, stage)
        row = jnp.sum(dots[stage], axis=0)[0:1, :]
        at = lax.broadcasted_iota(jnp.int32, row.shape, 1)
        return [jnp.sum(jnp.where(at == k, row, 0.0), axis=1, keepdims=True) for k in range(count)]

    def on(stage):
        return lambda place: halo[stage, place]

    shift = 0.25
    basis = [rhs]
    for k in range(BLOCK):
        image = operate(on(k + 1), shift)
        basis.append(image)
        if k < BLOCK - 1:
            landed(k + 2, spread(k + 2, image), image)
    count = 2 * BLOCK + 1
    publish(1, [basis[k // 2] * basis[(k + 1) // 2] for k in range(count)])
    listed = spread(BLOCK + 1, basis[BLOCK])
    landed(BLOCK + 1, listed, basis[BLOCK])
    basis.append(operate(on(BLOCK + 1), shift))
    first = gathered(1, count)
    moved, residual, direction, past = conjugate(
        ([0.0], [1.0]), ([0.0], [1.0]), (None, None, first), shift, BLOCK, True
    )
    step = combine(moved[1], basis)
    start_poly, before, size, ratio, turns = past
    for place in range(9):
        res[place] = combine(residual[1], [halo[k + 1, place] for k in range(BLOCK + 1)])

    later = turns
    chain = [res[place_of(0, 0)]]
    chain.append(operate(lambda place: res[place], later))
    listed = spread(BLOCK + 2, chain[1])
    lift = shift - later
    powers = [start_poly]
    for k in range(BLOCK - 1):
        powers.append(plus(lifted(powers[-1]), powers[-1], lift))
    olds = [combine(p, basis) for p in powers]
    twice = before
    for k in range(BLOCK - 1):
        twice = plus(lifted(twice), twice, lift)
    last = combine(twice, basis)
    pulls = [chain[0] + ratio * olds[0], chain[1] + ratio * olds[1]]
    landed(BLOCK + 2, listed, chain[1])
    chain.append(operate(on(BLOCK + 2), later))
    listed = spread(BLOCK + 3, chain[2])
    pulls.append(chain[2] + ratio * olds[2])
    old = (last - chain[2]) / size - later * olds[2]
    landed(BLOCK + 3, listed, chain[2])
    pulls.append(operate(on(BLOCK + 3), later) + ratio * old)
    count = 2 * BLOCK
    products = [pulls[k // 2] * pulls[(k + 1) // 2] for k in range(count)]
    products += [pulls[(k + 1) // 2] * chain[k // 2] for k in range(count - 1)]
    products += [chain[k // 2] * chain[(k + 1) // 2] for k in range(count - 2)]
    publish(2, products)
    second = gathered(2, len(products))
    seconds = (second[:count], second[count : 2 * count - 1], second[2 * count - 1 :])
    moved, _, _, _ = conjugate(([0.0], [1.0]), ([1.0], [0.0]), seconds, later, BLOCK, False)
    step = step + combine(moved[0], pulls) + combine(moved[1], chain)
    step = step * scale

    result = tiles[0] + step
    for j in range(COMPS):
        out_field[j, 0] = result[j * rows : (j + 1) * rows]
    for listed in copies:
        sent(listed)
    for stage in range(3):
        shared(dot_send, stage)
    store.wait()


def body(slabs, planes, images, shifts, initial_displacement):
    _, zs, ys, xs = images.shape
    layers, rows, across = shifts.shape[1:]
    elem = xs // across
    assert layers == 1 and zs == elem and elem == TILE and 4 * rows == TILE
    devices = slabs * planes
    parts, arrays = matrices(elem, rows, across)
    total = parts[-1][0] + parts[-1][1] + TILE
    vmem = pl.BlockSpec(memory_space=pltpu.VMEM)
    hbm = pl.BlockSpec(memory_space=pltpu.HBM)
    stages = ITERS + 1
    dma = pltpu.SemaphoreType.DMA

    def held(*shape):
        return pltpu.VMEM(shape, F32)

    return pl.pallas_call(
        functools.partial(kernel, slabs, planes, parts),
        out_shape=(
            jax.ShapeDtypeStruct(initial_displacement.shape, F32),
            jax.ShapeDtypeStruct(images.shape[1:], F32),
        ),
        in_specs=[hbm] * (3 + len(arrays)),
        out_specs=(vmem, hbm),
        scratch_shapes=[
            held(zs + 4, ys + 2 * TILE, xs),
            held(zs + 2, ys + 2 * TILE, xs),
            held(2, 3 * zs, xs),
            held(2, 3 * zs, xs),
            held(4, zs, xs),
            held(stages, TILE, across),
            held(stages, 9, TILE, across),
            held(3, devices, 2, across),
            held(COMPS, zs, ys, xs),
            held(zs, ys, xs),
            held(4 * TILE, xs),
            held(3, TILE, xs),
            held(len(PAIRS) * 3 * ys, xs),
            held(COMPS * 2 * ys, xs),
            held(total, 2 * across),
            held(total, 2 * across),
            held(COMPS * 9 * TILE + TILE, 2 * across),
            held(9, TILE, across),
            pltpu.VMEM(shifts.shape, jnp.int32),
            held(*initial_displacement.shape),
            *[held(*a.shape) for a in arrays],
            dma((2,)),
            dma((2 + len(arrays),)),
            dma,
            dma((2, 2)),
            dma((2, 2)),
            dma((2,)),
            dma((2,)),
            dma((4,)),
            dma((4,)),
            dma((stages, 8)),
            dma((stages, 8)),
            dma((3,)),
            dma((3,)),
            dma((3,)),
            dma((3,)),
        ],
        compiler_params=pltpu.CompilerParams(
            collective_id=0, has_side_effects=True, vmem_limit_bytes=56 * 1024 * 1024
        ),
        name="gauss_newton_step",
    )(images, shifts, initial_displacement, *[jnp.asarray(a) for a in arrays])


def solution(mesh):
    in_specs = (
        P(None, "slab", "plane", None),
        P(None, "slab", "plane", None),
        P(None, "slab", "plane", None),
    )
    out_specs = (P(None, "slab", "plane", None), P("slab", "plane", None))
    run = functools.partial(body, mesh.shape["slab"], mesh.shape["plane"])
    return jax.shard_map(run, mesh=mesh, in_specs=in_specs, out_specs=out_specs, check_vma=False)
```

```python
import functools

import jax
import jax.numpy as jnp
import numpy as np
from jax import lax
from jax.experimental import pallas as pl
from jax.experimental.pallas import tpu as pltpu
from jax.sharding import PartitionSpec as P

ITERS = 6
BLOCK = ITERS // 2
SPREAD = 128.0
reg_weight = 4.0

MESH = pl.DeviceIdType.MESH
F32 = jnp.float32
BF16 = jnp.bfloat16
TILE = 8
COMPS = 3
PAIRS = ((0, 0), (0, 1), (0, 2), (1, 1), (1, 2), (2, 2))
AROUND = tuple((dz, dy) for dz in (-1, 0, 1) for dy in (-1, 0, 1) if (dz, dy) != (0, 0))


def place_of(dz, dy):
    return (dz + 1) * 3 + dy + 1


def pair_of(i, j):
    return PAIRS.index((min(i, j), max(i, j)))


def matrices(elem, rows, across):
    w = np.arange(elem) / elem
    squares = ((1 - w) ** 2, w * (1 - w), w**2)
    count = elem * across
    hats = np.zeros((count, across))
    stencil = np.zeros((count, 2 * across))
    spread = np.zeros((across, count))
    for e in range(across):
        at = slice(e * elem, (e + 1) * elem)
        spread[e, at] = 1
        hats[at, e] = 1 - w
        stencil[at, e] += squares[0]
        if e + 1 < across:
            hats[at, e + 1] = w
            stencil[at, e + 1] += squares[2]
            stencil[at, across + e] = squares[1]

    height = rows * elem
    depth = len(PAIRS) * 3 * height

    def column(ij, cz, row):
        start = (ij * 3 + cz) * height + row * elem
        return slice(start, start + elem)

    last = rows - 1
    slab_rows = [(ij, cz, cy, r) for ij in range(6) for cz in (1, 2) for cy in range(3) for r in range(rows)]
    plane_rows = [(ij, cz, cy, last) for ij in range(6) for cz in (0, 1) for cy in (1, 2)]
    diag_rows = [(ij, cz, cy, last) for ij in range(6) for cz in (1, 2) for cy in (1, 2)]
    parts = []
    start = 0
    for listed in (slab_rows, plane_rows, diag_rows):
        used = -(-len(listed) // TILE) * TILE
        parts.append((start, used))
        start += used + TILE
    total = start
    send = np.zeros((total, depth))
    index = [{}, {}, {}]
    for part, listed in enumerate((slab_rows, plane_rows, diag_rows)):
        for n, key in enumerate(listed):
            ij, cz, cy, r = key
            send[parts[part][0] + n, column(ij, cz, r)] = squares[cy]
            index[part][key] = parts[part][0] + n

    own = np.zeros((COMPS * 9 * TILE + TILE, depth))
    came = np.zeros((COMPS * 9 * TILE + TILE, total))
    for i in range(COMPS):
        for dz in (-1, 0, 1):
            for dy in (-1, 0, 1):
                for j in range(COMPS):
                    for r in range(rows):
                        out = (i * 9 + place_of(dz, dy)) * TILE + j * rows + r
                        ij = pair_of(i, j)
                        layers = {0: ((0, 0), (-1, 2)), 1: ((0, 1),), -1: ((-1, 1),)}[dz]
                        lines = {0: ((r, 0), (r - 1, 2)), 1: ((r, 1),), -1: ((r - 1, 1),)}[dy]
                        for layer, cz in layers:
                            for line, cy in lines:
                                if layer == 0 and line >= 0:
                                    own[out, column(ij, cz, line)] = squares[cy]
                                elif layer < 0 and line >= 0:
                                    came[out, index[0][(ij, cz, cy, line)]] = 1
                                elif layer == 0:
                                    came[out, index[1][(ij, cz, cy, last)]] = 1
                                else:
                                    came[out, index[2][(ij, cz, cy, last)]] = 1

    loads = np.zeros((4 * TILE, COMPS * 2 * height))

    def line_of(i, cz, row):
        start = (i * 2 + cz) * height + row * elem
        return slice(start, start + elem)

    for i in range(COMPS):
        for r in range(rows):
            out = i * rows + r
            for cz in (0, 1):
                loads[cz * TILE + out, line_of(i, cz, r)] = 1 - w
                if r > 0:
                    loads[cz * TILE + out, line_of(i, cz, r - 1)] = w
        for cz in (0, 1):
            loads[(2 + cz) * TILE + i * rows, line_of(i, cz, last)] = w
    rise = np.zeros((COMPS, elem, height, 4 * TILE))
    for j in range(COMPS):
        for z in range(elem):
            for y in range(height):
                for dz, wz in ((0, 1 - w[z]), (1, w[z])):
                    for up, wy in ((0, 1 - w[y % elem]), (1, w[y % elem])):
                        line = y // elem + up
                        at = (dz * 2 + line // rows) * TILE + j * rows + line % rows
                        rise[j, z, y, at] += wz * wy
    rise = rise.reshape(-1, 4 * TILE)
    arrays = (stencil, hats, hats.T, spread, send, own, came, loads, rise)
    return parts, [np.asarray(a, dtype=np.float32) for a in arrays]


def split(x):
    high = x.astype(BF16)
    return high, (x - high.astype(F32)).astype(BF16)


def dot(a, b):
    return jnp.dot(a, b, preferred_element_type=F32)


def dot_left(x, exact):
    high, low = split(x)
    return dot(high, exact) + dot(low, exact)


def dot_right(exact, x):
    high, low = split(x)
    return dot(exact, high) + dot(exact, low)


def times(a, b):
    if isinstance(a, float) and a == 0.0 or isinstance(b, float) and b == 0.0:
        return 0.0
    if isinstance(a, float) and a == 1.0:
        return b
    if isinstance(b, float) and b == 1.0:
        return a
    return a * b


def total(a, b):
    if isinstance(a, float) and a == 0.0:
        return b
    if isinstance(b, float) and b == 0.0:
        return a
    return a + b


def lifted(poly):
    return [0.0] + list(poly)


def plus(a, b, factor):
    out = list(a) + [0.0] * (len(b) - len(a))
    for k, value in enumerate(b):
        out[k] = total(out[k], times(factor, value))
    return out


def product(a, b):
    out = [0.0] * (len(a) + len(b) - 1)
    for i, x in enumerate(a):
        for j, y in enumerate(b):
            out[i + j] = total(out[i + j], times(x, y))
    return out


def combine(poly, values):
    out = 0.0
    for k, value in enumerate(poly):
        if not (isinstance(value, float) and value == 0.0):
            out = total(out, times(value, values[k]))
    return out


def inner(x, y, moments):
    out = combine(product(x[0], y[0]), moments[0])
    mixed = plus(product(x[0], y[1]), product(x[1], y[0]), 1.0)
    out = total(out, combine(mixed, moments[1]))
    return total(out, combine(product(x[1], y[1]), moments[2]))


def conjugate(residual, direction, moments, shift, steps, go_on):
    moved = ([0.0], [0.0])
    norm = inner(residual, residual, moments)
    turns = 0.0
    past = None
    for k in range(steps):
        image = tuple(plus(lifted(d), d, shift) for d in direction)
        bend = inner(direction, image, moments)
        size = norm / bend
        moved = tuple(plus(m, d, size) for m, d in zip(moved, direction))
        if k == steps - 1 and not go_on:
            break
        before, old = residual, direction
        residual = tuple(plus(r, i, -size) for r, i in zip(residual, image))
        fresh = inner(residual, residual, moments)
        ratio = fresh / norm
        direction = tuple(plus(r, d, ratio) for r, d in zip(residual, direction))
        turns = total(turns, (bend / norm) * (1.0 / steps))
        norm = fresh
        past = (old[1], before[1], size, ratio, turns)
    return moved, residual, direction, past


def kernel(
    slabs,
    planes,
    parts,
    images,
    shifts_in,
    start_in,
    w_stencil_in,
    w_hats_in,
    w_nodes_in,
    w_spread_in,
    w_send_in,
    w_own_in,
    w_came_in,
    w_loads_in,
    w_rise_in,
    out_step,
    out_model,
    ref_ext,
    def_ext,
    def_side,
    pack,
    got_rows,
    got_diag,
    tiles,
    halo,
    dots,
    grads,
    model,
    moved,
    moves,
    moments,
    loads,
    send_buf,
    got_buf,
    coefs,
    res,
    shifts,
    start_field,
    w_stencil,
    w_hats,
    w_nodes,
    w_spread,
    w_send,
    w_own,
    w_came,
    w_loads,
    w_rise,
    load_sem,
    const_sem,
    out_sem,
    face_send,
    face_recv,
    row_send,
    row_recv,
    diag_send,
    diag_recv,
    tile_send,
    tile_recv,
    dot_send,
    dot_recv,
    part_send,
    part_recv,
):
    _, zs, ys, xs = images.shape
    rows, across = shifts_in.shape[2], shifts_in.shape[3]
    elem = xs // across
    devices = slabs * planes
    slab, plane = lax.axis_index("slab"), lax.axis_index("plane")
    me = slab * planes + plane

    def present(dz, dy):
        ok = None
        for d, at, count in ((dz, slab, slabs), (dy, plane, planes)):
            if d:
                here = at < count - 1 if d > 0 else at > 0
                ok = here if ok is None else jnp.logical_and(ok, here)
        return ok

    def beside(dz, dy):
        return (slab + dz, plane + dy)

    plane_to = [plane] + [jnp.where(plane + k < planes, plane + k, plane + k - planes) for k in range(1, planes)]

    def everyone(action):
        for to in plane_to[1:]:
            action((slab, to))

        def there(k, carry):
            at = jnp.where(slab + k < slabs, slab + k, slab + k - slabs)
            for to in plane_to:
                action((at, to))
            return carry

        lax.fori_loop(1, slabs, there, 0)

    mine = [
        pltpu.make_async_copy(images.at[0], ref_ext.at[pl.ds(2, zs), pl.ds(TILE, ys)], load_sem.at[0]),
        pltpu.make_async_copy(images.at[1], def_ext.at[pl.ds(1, zs), pl.ds(TILE, ys)], load_sem.at[1]),
    ]
    small = [
        pltpu.make_async_copy(src, dst, const_sem.at[n])
        for n, (src, dst) in enumerate(
            (
                (start_in, start_field),
                (shifts_in, shifts),
                (w_spread_in, w_spread),
                (w_nodes_in, w_nodes),
                (w_stencil_in, w_stencil),
                (w_hats_in, w_hats),
                (w_loads_in, w_loads),
                (w_send_in, w_send),
                (w_own_in, w_own),
                (w_came_in, w_came),
                (w_rise_in, w_rise),
            )
        )
    ]
    for copy in mine + small:
        copy.start()
    halo[...] = jnp.zeros(halo.shape, F32)
    tiles[...] = jnp.zeros(tiles.shape, F32)
    got_buf[...] = jnp.zeros(got_buf.shape, F32)
    barrier = pltpu.get_barrier_semaphore()
    everyone(lambda to: pl.semaphore_signal(barrier, inc=1, device_id=to, device_id_type=MESH))
    for copy in small[:1] + mine:
        copy.wait()
    for j in range(COMPS):
        tiles[0, j * rows : (j + 1) * rows, :] = start_field[j, 0]

    for side, (far, near) in enumerate(((1, 0), (ys - 2, ys - 1))):
        pack[side, 0:zs, :] = ref_ext[2 : 2 + zs, TILE + far, :]
        pack[side, zs : 2 * zs, :] = ref_ext[2 : 2 + zs, TILE + near, :]
        pack[side, 2 * zs :, :] = def_ext[1 : 1 + zs, TILE + near, :]
    pl.semaphore_wait(barrier, devices - 1)

    def remote(src, dst, send, recv, to):
        return pltpu.make_async_remote_copy(
            src_ref=src, dst_ref=dst, send_sem=send, recv_sem=recv, device_id=to, device_id_type=MESH
        )

    def faces():
        out = []
        for n, d in enumerate((-1, 1)):
            low = 0 if d < 0 else zs - 2
            here = ref_ext.at[pl.ds(2 + low, 2), pl.ds(TILE, ys)]
            there = ref_ext.at[pl.ds(2 + zs if d < 0 else 0, 2), pl.ds(TILE, ys)]
            out.append(((d, 0), remote(here, there, face_send.at[n, 0], face_recv.at[n, 0], beside(d, 0))))
            low = 0 if d < 0 else zs - 1
            here = def_ext.at[pl.ds(1 + low, 1), pl.ds(TILE, ys)]
            there = def_ext.at[pl.ds(1 + zs if d < 0 else 0, 1), pl.ds(TILE, ys)]
            out.append(((d, 0), remote(here, there, face_send.at[n, 1], face_recv.at[n, 1], beside(d, 0))))
        for n, d in enumerate((-1, 1)):
            out.append(
                ((0, d), remote(pack.at[n], got_rows.at[n], row_send.at[n], row_recv.at[n], beside(0, d)))
            )
        for n, (dz, dy) in enumerate(((-1, -1), (-1, 1), (1, -1), (1, 1))):
            here = pack.at[(dy + 1) // 2, pl.ds(2 * zs, zs)]
            out.append(
                ((dz, dy), remote(here, got_diag.at[n], diag_send.at[n], diag_recv.at[n], beside(dz, dy)))
            )
        return out

    def around(stage):
        out = []
        for n, (dz, dy) in enumerate(AROUND):
            copy = remote(
                tiles.at[stage],
                halo.at[stage, place_of(-dz, -dy)],
                tile_send.at[stage, n],
                tile_recv.at[stage, n],
                beside(dz, dy),
            )
            out.append(((dz, dy), copy))
        return out

    def begin(copies):
        for (dz, dy), copy in copies:
            pl.when(present(dz, dy))(copy.start)

    def arrive(copies):
        for (dz, dy), copy in copies:
            pl.when(present(-dz, -dy))(copy.wait_recv)

    def sent(copies):
        for (dz, dy), copy in copies:
            pl.when(present(dz, dy))(copy.wait_send)

    def share(stage):
        slot = dots.at[stage, me]
        everyone(lambda to: remote(slot, slot, dot_send.at[stage], dot_recv.at[stage], to).start())

    def shared(sem, stage):
        some = dots.at[stage, pl.ds(0, devices - 1)]
        pltpu.make_async_copy(some, some, sem.at[stage]).wait()

    def totals(stage):
        shared(dot_recv, stage)
        lanes = jnp.sum(dots[stage], axis=0)
        return jnp.sum(lanes, axis=1, keepdims=True)

    image_copies = faces()
    start_copies = around(0)
    begin(image_copies[:4])
    begin(start_copies)
    begin(image_copies[4:])
    for copy in small[1:]:
        copy.wait()

    codes = jnp.concatenate([shifts[j, 0] for j in range(COMPS)], axis=0).astype(F32).astype(BF16)
    wide = dot(codes, w_spread[...].astype(BF16))
    for n, dx in enumerate((-1, 0, 1)):
        moves[n, 0 : COMPS * rows, :] = pltpu.roll(wide, dx % xs, 1) if dx else wide

    arrive(start_copies)
    halo[0, place_of(0, 0)] = tiles[0]
    corner = jnp.concatenate([halo[0, place_of(dz, dy)] for dz in (0, 1) for dy in (0, 1)], axis=0)
    moved[...] = dot_right(w_rise[...].astype(BF16), dot_left(corner, w_nodes[...].astype(BF16)))

    arrive(image_copies[4:6])

    def clear(dz, dy, *views):
        def run():
            for ref, index in views:
                ref[index] = jnp.zeros(ref[index].shape, F32)

        pl.when(jnp.logical_not(present(dz, dy)))(run)

    for n, d in enumerate((1, -1)):
        clear(0, d, (got_rows, (n,)))
    top = TILE + ys
    ref_ext[2 : 2 + zs, top, :] = got_rows[0, zs : 2 * zs, :]
    ref_ext[2 : 2 + zs, top + 1, :] = got_rows[0, 0:zs, :]
    def_ext[1 : 1 + zs, top, :] = got_rows[0, 2 * zs :, :]
    ref_ext[2 : 2 + zs, TILE - 2, :] = got_rows[1, 0:zs, :]
    ref_ext[2 : 2 + zs, TILE - 1, :] = got_rows[1, zs : 2 * zs, :]
    def_ext[1 : 1 + zs, TILE - 1, :] = got_rows[1, 2 * zs :, :]
    def lean(z):
        for n, dy in enumerate((-1, 1)):
            def_side[n, z] = def_ext[z, TILE + dy : TILE + dy + ys, :]

    def lean_own(z, carry):
        lean(z)
        return carry

    lax.fori_loop(1, zs + 1, lean_own, 0)

    lane = lax.broadcasted_iota(jnp.int32, (TILE, xs), 1)

    def along(value, d):
        rolled = pltpu.roll(value, (-d) % xs, 1)
        inside = lane < xs - d if d > 0 else lane >= -d
        return jnp.where(inside, rolled, 0.0)

    def moved_at(j, z, r):
        return moved[pl.ds(pl.multiple_of((j * zs + z) * ys + r * elem, elem), elem), :]

    def flat(z, carry):
        for r in range(rows):
            base = TILE + r * elem

            def ref(dy):
                return ref_ext[z + 2, base + dy : base + dy + elem, :]

            centre = ref(0)
            gy = (ref(-2) - ref(2) + 8.0 * (ref(1) - ref(-1))) * (1.0 / 12.0)
            gx = along(centre, -2) - along(centre, 2) + 8.0 * (along(centre, 1) - along(centre, -1))
            gx = gx * (1.0 / 12.0)
            here = slice(r * elem, (r + 1) * elem)
            grads[1, z, here, :] = gy
            grads[2, z, here, :] = gx
            model[z, here, :] = gy * moved_at(1, z, r) + gx * moved_at(2, z, r)
        return carry

    def deep(z, carry):
        for r in range(rows):
            base = TILE + r * elem

            def ref(dz):
                return ref_ext[z + (2 + dz), base : base + elem, :]

            gz = (ref(-2) - ref(2) + 8.0 * (ref(1) - ref(-1))) * (1.0 / 12.0)
            here = slice(r * elem, (r + 1) * elem)
            grads[0, z, here, :] = gz
            model[z, here, :] = model[z, here, :] + gz * moved_at(0, z, r)
        return carry

    def warp(z, carry):
        for r in range(rows):
            here = slice(r * elem, (r + 1) * elem)
            warped = None
            for n, dx in enumerate((-1, 0, 1)):
                s = [moves[n, j * rows + r : j * rows + r + 1, :] for j in range(2)]
                s = [jnp.broadcast_to(v, (elem, xs)) for v in s]
                below, above = s[0] < -0.5, s[0] > 0.5
                line = []
                for dy in (-1, 0, 1):

                    def layer(dz):
                        if dy == 0:
                            return def_ext[z + 1 + dz, TILE + r * elem : TILE + (r + 1) * elem, :]
                        return def_side[(dy + 1) // 2, z + 1 + dz, here, :]

                    value = jnp.where(below, layer(-1), layer(0))
                    line.append(jnp.where(above, layer(1), value))
                value = jnp.where(s[1] < -0.5, line[0], line[1])
                value = jnp.where(s[1] > 0.5, line[2], value)
                if dx:
                    value = along(value, dx)
                if warped is None:
                    warped = value
                else:
                    sx = jnp.broadcast_to(moves[1, 2 * rows + r : 2 * rows + r + 1, :], (elem, xs))
                    warped = jnp.where(sx > dx - 0.5, value, warped)
            model[z, here, :] = model[z, here, :] + warped
        return carry

    lax.fori_loop(0, zs, flat, 0)
    lax.fori_loop(1, zs - 1, warp, 0)
    lax.fori_loop(2, zs - 2, deep, 0)
    arrive(image_copies[:4] + image_copies[6:])
    clear(-1, 0, (ref_ext, (slice(0, 2),)), (def_ext, (slice(0, 1),)))
    clear(1, 0, (ref_ext, (slice(2 + zs, 4 + zs),)), (def_ext, (slice(1 + zs, 2 + zs),)))
    for n, (dz, dy) in enumerate(((1, 1), (1, -1), (-1, 1), (-1, -1))):
        clear(dz, dy, (got_diag, (n,)))
    def_ext[1 + zs, top : top + 1, :] = got_diag[0, 0:1, :]
    def_ext[1 + zs, TILE - 1 : TILE, :] = got_diag[1, 0:1, :]
    def_ext[0, top : top + 1, :] = got_diag[2, zs - 1 : zs, :]
    def_ext[0, TILE - 1 : TILE, :] = got_diag[3, zs - 1 : zs, :]
    lean(0)
    lean(zs + 1)
    warp(0, 0)
    warp(zs - 1, 0)
    for z in (0, 1, zs - 2, zs - 1):
        deep(z, 0)
    store = pltpu.make_async_copy(model, out_model, out_sem)
    store.start()

    width = across
    lines = xs // width

    def gather(n, carry):
        r, c = lax.div(n, lines), lax.rem(n, lines)
        ay = pl.ds(pl.multiple_of(r * elem, elem), elem)
        ax = pl.ds(pl.multiple_of(c * width, width), width)
        sums = [[None] * 3 for _ in PAIRS]
        forces = [[None] * 2 for _ in range(COMPS)]

        def add(total, weight, value):
            if weight == 0.0:
                return total
            term = value if weight == 1.0 else weight * value
            return term if total is None else total + term

        for z in range(zs):
            w = z / elem
            g = [grads[j, z, ay, ax] for j in range(COMPS)]
            q = ref_ext[2 + z, pl.ds(pl.multiple_of(TILE + r * elem, elem), elem), ax] - model[z, ay, ax]
            for ij, (i, j) in enumerate(PAIRS):
                product = g[i] * g[j]
                if i == j:
                    carry = carry + product
                for cz, weight in enumerate(((1 - w) ** 2, w * (1 - w), w * w)):
                    sums[ij][cz] = add(sums[ij][cz], weight, product)
            for i in range(COMPS):
                product = g[i] * q
                for cz, weight in enumerate((1 - w, w)):
                    forces[i][cz] = add(forces[i][cz], weight, product)
        for ij in range(len(PAIRS)):
            for cz in range(3):
                at = pl.multiple_of((ij * 3 + cz) * ys + r * elem, elem)
                moments[pl.ds(at, elem), ax] = sums[ij][cz]
        for i in range(COMPS):
            for cz in range(2):
                at = pl.multiple_of((i * 2 + cz) * ys + r * elem, elem)
                loads[pl.ds(at, elem), ax] = forces[i][cz]
        return carry

    energy = lax.fori_loop(0, rows * lines, gather, jnp.zeros((elem, width), F32))
    dots[0, me] = jnp.zeros(dots.shape[2:], F32)
    dots[0, me, 0:1, :] = jnp.sum(energy, axis=0, keepdims=True)
    share(0)
    summed = dot_left(moments[...], w_stencil[...].astype(BF16))
    load_tiles = dot_right(w_loads[...].astype(BF16), dot_left(loads[...], w_hats[...].astype(BF16)))
    send_buf[...] = dot_right(w_send[...].astype(BF16), summed)
    for (start, used), n in zip(parts, (1, 2, 3)):
        send_buf[start + used : start + used + TILE, :across] = load_tiles[n * TILE : (n + 1) * TILE]
    part_copies = []
    for n, ((start, used), to) in enumerate(zip(parts, ((1, 0), (0, 1), (1, 1)))):
        at = pl.ds(start, used + TILE)
        part_copies.append(
            (to, remote(send_buf.at[at], got_buf.at[at], part_send.at[n], part_recv.at[n], beside(*to)))
        )
    begin(part_copies)
    coefs[...] = dot_right(w_own[...].astype(BF16), summed)

    node_lane = lax.broadcasted_iota(jnp.int32, (TILE, across), 1)
    sub = lax.broadcasted_iota(jnp.int32, (TILE, across), 0)
    line = lax.rem(sub, rows)
    group = lax.div(sub, rows)

    def neighbour(get, dz, dy):
        centre = get(place_of(dz, 0))
        if dy == 0:
            return centre
        edge = get(place_of(dz, dy))
        inner = pltpu.roll(centre, (-dy) % TILE, 0)
        outer = pltpu.roll(edge, (dy * (rows - 1)) % TILE, 0)
        return jnp.where(line == (rows - 1 if dy > 0 else 0), outer, inner)

    def start_at(place):
        return halo[0, place]

    centre = start_at(place_of(0, 0))
    lap = 6.0 * centre - neighbour(start_at, -1, 0) - neighbour(start_at, 1, 0)
    lap = lap - neighbour(start_at, 0, -1) - neighbour(start_at, 0, 1)
    lap = lap - jnp.where(node_lane > 0, pltpu.roll(centre, 1, 1), 0.0)
    lap = lap - jnp.where(node_lane < across - 1, pltpu.roll(centre, across - 1, 1), 0.0)
    lap = jnp.where(group < COMPS, lap, 0.0)

    penalty = totals(0)[0:1, :] * (reg_weight / (devices * zs * ys * xs))
    arrive(part_copies)
    rhs = load_tiles[0:TILE] - penalty * lap
    for start, used in parts:
        rhs = rhs + got_buf[start + used : start + used + TILE, :across]
    tiles[1] = rhs
    rhs_copies = around(1)
    begin(rhs_copies)

    coefs[...] = coefs[...] + dot_right(w_came[...].astype(BF16), got_buf[...])
    for i in range(COMPS):
        same = jnp.where(group == i, 1.0, 0.0) * penalty

        def raise_by(dz, dy, part, value):
            at = pl.ds((i * 9 + place_of(dz, dy)) * TILE, TILE)
            to = pl.ds(part * across, across)
            coefs[at, to] = coefs[at, to] + value

        raise_by(0, 0, 0, 6.0 * same)
        raise_by(0, 0, 1, jnp.where(node_lane < across - 1, -same, 0.0))
        for dz, dy in ((-1, 0), (1, 0), (0, -1), (0, 1)):
            raise_by(dz, dy, 0, -same)

    arrive(rhs_copies)
    halo[1, place_of(0, 0)] = rhs
    scale = 1.0 / (penalty * SPREAD)

    def operate(get, shift):
        out = [None] * COMPS
        back = [None] * COMPS
        for dz in (-1, 0, 1):
            for dy in (-1, 0, 1):
                v = neighbour(get, dz, dy)
                ahead = pltpu.roll(v, across - 1, 1)
                for i in range(COMPS):
                    at = pl.ds((i * 9 + place_of(dz, dy)) * TILE, TILE)
                    here, link = coefs[at, 0:across], coefs[at, across : 2 * across]
                    term = here * v + link * ahead
                    out[i] = term if out[i] is None else out[i] + term
                    term = link * v
                    back[i] = term if back[i] is None else back[i] + term
        image = jnp.zeros((TILE, across), F32)
        for i in range(COMPS):
            value = out[i] + pltpu.roll(back[i], 1, 1)
            value = value + pltpu.roll(value, TILE // 2, 0)
            value = value + pltpu.roll(value, rows, 0)
            image = jnp.where(group == i, value, image)
        return image * scale - shift * get(place_of(0, 0))

    copies = [image_copies, start_copies, part_copies, rhs_copies]

    def spread(stage, image):
        tiles[stage] = image
        listed = around(stage)
        begin(listed)
        copies.append(listed)
        return listed

    def landed(stage, listed, image):
        arrive(listed)
        halo[stage, place_of(0, 0)] = image

    def publish(stage, products):
        lines = [jnp.sum(p, axis=0, keepdims=True) for p in products]
        fill = -len(lines) % TILE
        lines += [jnp.zeros((1, across), F32)] * fill
        stacked = jnp.concatenate(lines, axis=0)
        column = jnp.sum(stacked, axis=1, keepdims=True)
        at = lax.broadcasted_iota(jnp.int32, stacked.shape, 0) == lax.broadcasted_iota(jnp.int32, stacked.shape, 1)
        dots[stage, me] = jnp.zeros(dots.shape[2:], F32)
        dots[stage, me, 0:1, :] = jnp.sum(jnp.where(at, column, 0.0), axis=0, keepdims=True)
        share(stage)

    def gathered(stage, count):
        shared(dot_recv, stage)
        row = jnp.sum(dots[stage], axis=0)[0:1, :]
        at = lax.broadcasted_iota(jnp.int32, row.shape, 1)
        return [jnp.sum(jnp.where(at == k, row, 0.0), axis=1, keepdims=True) for k in range(count)]

    def on(stage):
        return lambda place: halo[stage, place]

    shift = 0.25
    basis = [rhs]
    for k in range(BLOCK):
        image = operate(on(k + 1), shift)
        basis.append(image)
        if k < BLOCK - 1:
            landed(k + 2, spread(k + 2, image), image)
    count = 2 * BLOCK + 1
    publish(1, [basis[k // 2] * basis[(k + 1) // 2] for k in range(count)])
    listed = spread(BLOCK + 1, basis[BLOCK])
    landed(BLOCK + 1, listed, basis[BLOCK])
    basis.append(operate(on(BLOCK + 1), shift))
    first = gathered(1, count)
    moved, residual, direction, past = conjugate(
        ([0.0], [1.0]), ([0.0], [1.0]), (None, None, first), shift, BLOCK, True
    )
    step = combine(moved[1], basis)
    start_poly, before, size, ratio, turns = past
    for place in range(9):
        res[place] = combine(residual[1], [halo[k + 1, place] for k in range(BLOCK + 1)])

    later = turns
    chain = [res[place_of(0, 0)]]
    chain.append(operate(lambda place: res[place], later))
    listed = spread(BLOCK + 2, chain[1])
    lift = shift - later
    powers = [start_poly]
    for k in range(BLOCK - 1):
        powers.append(plus(lifted(powers[-1]), powers[-1], lift))
    olds = [combine(p, basis) for p in powers]
    twice = before
    for k in range(BLOCK - 1):
        twice = plus(lifted(twice), twice, lift)
    last = combine(twice, basis)
    pulls = [chain[0] + ratio * olds[0], chain[1] + ratio * olds[1]]
    landed(BLOCK + 2, listed, chain[1])
    chain.append(operate(on(BLOCK + 2), later))
    listed = spread(BLOCK + 3, chain[2])
    pulls.append(chain[2] + ratio * olds[2])
    old = (last - chain[2]) / size - later * olds[2]
    landed(BLOCK + 3, listed, chain[2])
    pulls.append(operate(on(BLOCK + 3), later) + ratio * old)
    count = 2 * BLOCK
    products = [pulls[k // 2] * pulls[(k + 1) // 2] for k in range(count)]
    products += [pulls[(k + 1) // 2] * chain[k // 2] for k in range(count - 1)]
    products += [chain[k // 2] * chain[(k + 1) // 2] for k in range(count - 2)]
    publish(2, products)
    second = gathered(2, len(products))
    seconds = (second[:count], second[count : 2 * count - 1], second[2 * count - 1 :])
    moved, _, _, _ = conjugate(([0.0], [1.0]), ([1.0], [0.0]), seconds, later, BLOCK, False)
    step = step + combine(moved[0], pulls) + combine(moved[1], chain)
    step = step * scale

    for j in range(COMPS):
        out_step[j, 0] = step[j * rows : (j + 1) * rows]
    for listed in copies:
        sent(listed)
    for stage in range(3):
        shared(dot_send, stage)
    store.wait()


def body(slabs, planes, images, shifts, initial_displacement):
    _, zs, ys, xs = images.shape
    layers, rows, across = shifts.shape[1:]
    elem = xs // across
    assert layers == 1 and zs == elem and elem == TILE and 4 * rows == TILE
    devices = slabs * planes
    parts, arrays = matrices(elem, rows, across)
    total = parts[-1][0] + parts[-1][1] + TILE
    vmem = pl.BlockSpec(memory_space=pltpu.VMEM)
    hbm = pl.BlockSpec(memory_space=pltpu.HBM)
    stages = ITERS + 1
    dma = pltpu.SemaphoreType.DMA

    def held(*shape):
        return pltpu.VMEM(shape, F32)

    step, model = pl.pallas_call(
        functools.partial(kernel, slabs, planes, parts),
        out_shape=(
            jax.ShapeDtypeStruct(initial_displacement.shape, F32),
            jax.ShapeDtypeStruct(images.shape[1:], F32),
        ),
        in_specs=[hbm] * (3 + len(arrays)),
        out_specs=(vmem, hbm),
        scratch_shapes=[
            held(zs + 4, ys + 2 * TILE, xs),
            held(zs + 2, ys + 2 * TILE, xs),
            held(2, zs + 2, ys, xs),
            held(2, 3 * zs, xs),
            held(2, 3 * zs, xs),
            held(4, zs, xs),
            held(stages, TILE, across),
            held(stages, 9, TILE, across),
            held(3, devices, 2, across),
            held(COMPS, zs, ys, xs),
            held(zs, ys, xs),
            held(COMPS * zs * ys, xs),
            held(3, TILE, xs),
            held(len(PAIRS) * 3 * ys, xs),
            held(COMPS * 2 * ys, xs),
            held(total, 2 * across),
            held(total, 2 * across),
            held(COMPS * 9 * TILE + TILE, 2 * across),
            held(9, TILE, across),
            pltpu.VMEM(shifts.shape, jnp.int32),
            held(*initial_displacement.shape),
            *[held(*a.shape) for a in arrays],
            dma((2,)),
            dma((2 + len(arrays),)),
            dma,
            dma((2, 2)),
            dma((2, 2)),
            dma((2,)),
            dma((2,)),
            dma((4,)),
            dma((4,)),
            dma((stages, 8)),
            dma((stages, 8)),
            dma((3,)),
            dma((3,)),
            dma((3,)),
            dma((3,)),
        ],
        compiler_params=pltpu.CompilerParams(
            collective_id=0, has_side_effects=True, vmem_limit_bytes=56 * 1024 * 1024
        ),
        name="gauss_newton_step",
    )(images, shifts, initial_displacement, *[jnp.asarray(a) for a in arrays])
    return initial_displacement + step, images[0] - model


def solution(mesh):
    in_specs = (
        P(None, "slab", "plane", None),
        P(None, "slab", "plane", None),
        P(None, "slab", "plane", None),
    )
    out_specs = (P(None, "slab", "plane", None), P("slab", "plane", None))
    run = functools.partial(body, mesh.shape["slab"], mesh.shape["plane"])
    return jax.shard_map(run, mesh=mesh, in_specs=in_specs, out_specs=out_specs, check_vma=False)
```

```python
import functools

import jax
import jax.numpy as jnp
import numpy as np
from jax import lax
from jax.experimental import pallas as pl
from jax.experimental.pallas import tpu as pltpu
from jax.sharding import PartitionSpec as P

ITERS = 6
BLOCK = ITERS // 2
SPREAD = 128.0
reg_weight = 4.0

MESH = pl.DeviceIdType.MESH
F32 = jnp.float32
BF16 = jnp.bfloat16
TILE = 8
COMPS = 3
PAIRS = ((0, 0), (0, 1), (0, 2), (1, 1), (1, 2), (2, 2))
AROUND = tuple((dz, dy) for dz in (-1, 0, 1) for dy in (-1, 0, 1) if (dz, dy) != (0, 0))


def place_of(dz, dy):
    return (dz + 1) * 3 + dy + 1


def pair_of(i, j):
    return PAIRS.index((min(i, j), max(i, j)))


def matrices(elem, rows, across):
    w = np.arange(elem) / elem
    squares = ((1 - w) ** 2, w * (1 - w), w**2)
    count = elem * across
    hats = np.zeros((count, across))
    stencil = np.zeros((count, 2 * across))
    spread = np.zeros((across, count))
    for e in range(across):
        at = slice(e * elem, (e + 1) * elem)
        spread[e, at] = 1
        hats[at, e] = 1 - w
        stencil[at, e] += squares[0]
        if e + 1 < across:
            hats[at, e + 1] = w
            stencil[at, e + 1] += squares[2]
            stencil[at, across + e] = squares[1]

    height = rows * elem
    depth = len(PAIRS) * 3 * height

    def column(ij, cz, row):
        start = (ij * 3 + cz) * height + row * elem
        return slice(start, start + elem)

    last = rows - 1
    slab_rows = [(ij, cz, cy, r) for ij in range(6) for cz in (1, 2) for cy in range(3) for r in range(rows)]
    plane_rows = [(ij, cz, cy, last) for ij in range(6) for cz in (0, 1) for cy in (1, 2)]
    diag_rows = [(ij, cz, cy, last) for ij in range(6) for cz in (1, 2) for cy in (1, 2)]
    parts = []
    start = 0
    for listed in (slab_rows, plane_rows, diag_rows):
        used = -(-len(listed) // TILE) * TILE
        parts.append((start, used))
        start += used + TILE
    total = start
    send = np.zeros((total, depth))
    index = [{}, {}, {}]
    for part, listed in enumerate((slab_rows, plane_rows, diag_rows)):
        for n, key in enumerate(listed):
            ij, cz, cy, r = key
            send[parts[part][0] + n, column(ij, cz, r)] = squares[cy]
            index[part][key] = parts[part][0] + n

    own = np.zeros((COMPS * 9 * TILE + TILE, depth))
    came = np.zeros((COMPS * 9 * TILE + TILE, total))
    for i in range(COMPS):
        for dz in (-1, 0, 1):
            for dy in (-1, 0, 1):
                for j in range(COMPS):
                    for r in range(rows):
                        out = (i * 9 + place_of(dz, dy)) * TILE + j * rows + r
                        ij = pair_of(i, j)
                        layers = {0: ((0, 0), (-1, 2)), 1: ((0, 1),), -1: ((-1, 1),)}[dz]
                        lines = {0: ((r, 0), (r - 1, 2)), 1: ((r, 1),), -1: ((r - 1, 1),)}[dy]
                        for layer, cz in layers:
                            for line, cy in lines:
                                if layer == 0 and line >= 0:
                                    own[out, column(ij, cz, line)] = squares[cy]
                                elif layer < 0 and line >= 0:
                                    came[out, index[0][(ij, cz, cy, line)]] = 1
                                elif layer == 0:
                                    came[out, index[1][(ij, cz, cy, last)]] = 1
                                else:
                                    came[out, index[2][(ij, cz, cy, last)]] = 1

    loads = np.zeros((4 * TILE, COMPS * 2 * height))

    def line_of(i, cz, row):
        start = (i * 2 + cz) * height + row * elem
        return slice(start, start + elem)

    for i in range(COMPS):
        for r in range(rows):
            out = i * rows + r
            for cz in (0, 1):
                loads[cz * TILE + out, line_of(i, cz, r)] = 1 - w
                if r > 0:
                    loads[cz * TILE + out, line_of(i, cz, r - 1)] = w
        for cz in (0, 1):
            loads[(2 + cz) * TILE + i * rows, line_of(i, cz, last)] = w
    rise = np.zeros((COMPS, elem, height, 4 * TILE))
    for j in range(COMPS):
        for z in range(elem):
            for y in range(height):
                for dz, wz in ((0, 1 - w[z]), (1, w[z])):
                    for up, wy in ((0, 1 - w[y % elem]), (1, w[y % elem])):
                        line = y // elem + up
                        at = (dz * 2 + line // rows) * TILE + j * rows + line % rows
                        rise[j, z, y, at] += wz * wy
    rise = rise.reshape(-1, 4 * TILE)
    arrays = (stencil, hats, hats.T, spread, send, own, came, loads, rise)
    return parts, [np.asarray(a, dtype=np.float32) for a in arrays]


def split(x):
    high = x.astype(BF16)
    return high, (x - high.astype(F32)).astype(BF16)


def dot(a, b):
    return jnp.dot(a, b, preferred_element_type=F32)


def dot_left(x, exact):
    high, low = split(x)
    return dot(high, exact) + dot(low, exact)


def dot_right(exact, x):
    high, low = split(x)
    return dot(exact, high) + dot(exact, low)


def times(a, b):
    if isinstance(a, float) and a == 0.0 or isinstance(b, float) and b == 0.0:
        return 0.0
    if isinstance(a, float) and a == 1.0:
        return b
    if isinstance(b, float) and b == 1.0:
        return a
    return a * b


def total(a, b):
    if isinstance(a, float) and a == 0.0:
        return b
    if isinstance(b, float) and b == 0.0:
        return a
    return a + b


def lifted(poly):
    return [0.0] + list(poly)


def plus(a, b, factor):
    out = list(a) + [0.0] * (len(b) - len(a))
    for k, value in enumerate(b):
        out[k] = total(out[k], times(factor, value))
    return out


def product(a, b):
    out = [0.0] * (len(a) + len(b) - 1)
    for i, x in enumerate(a):
        for j, y in enumerate(b):
            out[i + j] = total(out[i + j], times(x, y))
    return out


def combine(poly, values):
    out = 0.0
    for k, value in enumerate(poly):
        if not (isinstance(value, float) and value == 0.0):
            out = total(out, times(value, values[k]))
    return out


def inner(x, y, moments):
    out = combine(product(x[0], y[0]), moments[0])
    mixed = plus(product(x[0], y[1]), product(x[1], y[0]), 1.0)
    out = total(out, combine(mixed, moments[1]))
    return total(out, combine(product(x[1], y[1]), moments[2]))


def conjugate(residual, direction, moments, shift, steps, go_on):
    moved = ([0.0], [0.0])
    norm = inner(residual, residual, moments)
    turns = 0.0
    past = None
    for k in range(steps):
        image = tuple(plus(lifted(d), d, shift) for d in direction)
        bend = inner(direction, image, moments)
        size = norm / bend
        moved = tuple(plus(m, d, size) for m, d in zip(moved, direction))
        if k == steps - 1 and not go_on:
            break
        before, old = residual, direction
        residual = tuple(plus(r, i, -size) for r, i in zip(residual, image))
        fresh = inner(residual, residual, moments)
        ratio = fresh / norm
        direction = tuple(plus(r, d, ratio) for r, d in zip(residual, direction))
        turns = total(turns, (bend / norm) * (1.0 / steps))
        norm = fresh
        past = (old[1], before[1], size, ratio, turns)
    return moved, residual, direction, past


def kernel(
    slabs,
    planes,
    parts,
    images,
    shifts_in,
    start_in,
    w_stencil_in,
    w_hats_in,
    w_nodes_in,
    w_spread_in,
    w_send_in,
    w_own_in,
    w_came_in,
    w_loads_in,
    w_rise_in,
    out_field,
    out_mismatch,
    ref_ext,
    def_ext,
    def_side,
    pack,
    got_rows,
    got_diag,
    tiles,
    halo,
    row_dots,
    column_dots,
    grads,
    model,
    moved,
    moves,
    moments,
    loads,
    send_buf,
    got_buf,
    coefs,
    res,
    shifts,
    start_field,
    w_stencil,
    w_hats,
    w_nodes,
    w_spread,
    w_send,
    w_own,
    w_came,
    w_loads,
    w_rise,
    load_sem,
    const_sem,
    out_sem,
    face_send,
    face_recv,
    row_send,
    row_recv,
    diag_send,
    diag_recv,
    tile_send,
    tile_recv,
    dot_send,
    dot_recv,
    part_send,
    part_recv,
):
    _, zs, ys, xs = images.shape
    rows, across = shifts_in.shape[2], shifts_in.shape[3]
    elem = xs // across
    devices = slabs * planes
    slab, plane = lax.axis_index("slab"), lax.axis_index("plane")

    def present(dz, dy):
        ok = None
        for d, at, count in ((dz, slab, slabs), (dy, plane, planes)):
            if d:
                here = at < count - 1 if d > 0 else at > 0
                ok = here if ok is None else jnp.logical_and(ok, here)
        return ok

    def beside(dz, dy):
        return (slab + dz, plane + dy)

    def wrapped(at, k, count):
        return jnp.where(at + k < count, at + k, at + k - count)

    row_others = [(slab, wrapped(plane, k, planes)) for k in range(1, planes)]
    column_others = [(wrapped(slab, k, slabs), plane) for k in range(1, slabs)]
    corners = [(dz, dy) for dz, dy in AROUND if dz and dy]

    mine = [
        pltpu.make_async_copy(images.at[0], ref_ext.at[pl.ds(2, zs), pl.ds(TILE, ys)], load_sem.at[0]),
        pltpu.make_async_copy(images.at[1], def_ext.at[pl.ds(1, zs), pl.ds(TILE, ys)], load_sem.at[1]),
    ]
    small = [
        pltpu.make_async_copy(src, dst, const_sem.at[n])
        for n, (src, dst) in enumerate(
            (
                (start_in, start_field),
                (shifts_in, shifts),
                (w_spread_in, w_spread),
                (w_nodes_in, w_nodes),
                (w_stencil_in, w_stencil),
                (w_hats_in, w_hats),
                (w_loads_in, w_loads),
                (w_send_in, w_send),
                (w_own_in, w_own),
                (w_came_in, w_came),
                (w_rise_in, w_rise),
            )
        )
    ]
    for copy in mine + small:
        copy.start()
    halo[...] = jnp.zeros(halo.shape, F32)
    tiles[...] = jnp.zeros(tiles.shape, F32)
    got_buf[...] = jnp.zeros(got_buf.shape, F32)
    barrier = pltpu.get_barrier_semaphore()

    def greet(to):
        pl.semaphore_signal(barrier, inc=1, device_id=to, device_id_type=MESH)

    for to in row_others + column_others:
        greet(to)
    greeted = planes - 1 + slabs - 1
    for dz, dy in corners:
        pl.when(present(dz, dy))(functools.partial(greet, beside(dz, dy)))
        greeted = greeted + jnp.where(present(dz, dy), 1, 0)
    for copy in small[:1] + mine:
        copy.wait()
    for j in range(COMPS):
        tiles[0, j * rows : (j + 1) * rows, :] = start_field[j, 0]

    for side, (far, near) in enumerate(((1, 0), (ys - 2, ys - 1))):
        pack[side, 0:zs, :] = ref_ext[2 : 2 + zs, TILE + far, :]
        pack[side, zs : 2 * zs, :] = ref_ext[2 : 2 + zs, TILE + near, :]
        pack[side, 2 * zs :, :] = def_ext[1 : 1 + zs, TILE + near, :]
    pl.semaphore_wait(barrier, greeted)

    def remote(src, dst, send, recv, to):
        return pltpu.make_async_remote_copy(
            src_ref=src, dst_ref=dst, send_sem=send, recv_sem=recv, device_id=to, device_id_type=MESH
        )

    def faces():
        out = []
        for n, d in enumerate((-1, 1)):
            low = 0 if d < 0 else zs - 2
            here = ref_ext.at[pl.ds(2 + low, 2), pl.ds(TILE, ys)]
            there = ref_ext.at[pl.ds(2 + zs if d < 0 else 0, 2), pl.ds(TILE, ys)]
            out.append(((d, 0), remote(here, there, face_send.at[n, 0], face_recv.at[n, 0], beside(d, 0))))
            low = 0 if d < 0 else zs - 1
            here = def_ext.at[pl.ds(1 + low, 1), pl.ds(TILE, ys)]
            there = def_ext.at[pl.ds(1 + zs if d < 0 else 0, 1), pl.ds(TILE, ys)]
            out.append(((d, 0), remote(here, there, face_send.at[n, 1], face_recv.at[n, 1], beside(d, 0))))
        for n, d in enumerate((-1, 1)):
            out.append(
                ((0, d), remote(pack.at[n], got_rows.at[n], row_send.at[n], row_recv.at[n], beside(0, d)))
            )
        for n, (dz, dy) in enumerate(((-1, -1), (-1, 1), (1, -1), (1, 1))):
            here = pack.at[(dy + 1) // 2, pl.ds(2 * zs, zs)]
            out.append(
                ((dz, dy), remote(here, got_diag.at[n], diag_send.at[n], diag_recv.at[n], beside(dz, dy)))
            )
        return out

    def around(stage):
        out = []
        for n, (dz, dy) in enumerate(AROUND):
            copy = remote(
                tiles.at[stage],
                halo.at[stage, place_of(-dz, -dy)],
                tile_send.at[stage, n],
                tile_recv.at[stage, n],
                beside(dz, dy),
            )
            out.append(((dz, dy), copy))
        return out

    def begin(copies):
        for (dz, dy), copy in copies:
            pl.when(present(dz, dy))(copy.start)

    def arrive(copies):
        for (dz, dy), copy in copies:
            pl.when(present(-dz, -dy))(copy.wait_recv)

    def sent(copies):
        for (dz, dy), copy in copies:
            pl.when(present(dz, dy))(copy.wait_send)

    def share(stage, row):
        slot = row_dots.at[stage, plane]
        row_dots[stage, plane] = jnp.broadcast_to(row, row_dots.shape[2:])
        for to in row_others:
            remote(slot, slot, dot_send.at[stage, 0], dot_recv.at[stage, 0], to).start()

    def pass_on(stage):
        shared(dot_recv, stage, 0)
        slot = column_dots.at[stage, slab]
        column_dots[stage, slab] = jnp.sum(row_dots[stage], axis=0)
        for to in column_others:
            remote(slot, slot, dot_send.at[stage, 1], dot_recv.at[stage, 1], to).start()

    def shared(sem, stage, phase):
        held, count = ((row_dots, planes), (column_dots, slabs))[phase]
        if count > 1:
            some = held.at[stage, pl.ds(0, count - 1)]
            pltpu.make_async_copy(some, some, sem.at[stage, phase]).wait()

    def totals(stage):
        shared(dot_recv, stage, 1)
        return jnp.sum(column_dots[stage], axis=0)[0:1, :]

    image_copies = faces()
    start_copies = around(0)
    begin(image_copies[:4])
    begin(start_copies)
    begin(image_copies[4:])
    for copy in small[1:]:
        copy.wait()

    codes = jnp.concatenate([shifts[j, 0] for j in range(COMPS)], axis=0).astype(F32).astype(BF16)
    wide = dot(codes, w_spread[...].astype(BF16))
    for n, dx in enumerate((-1, 0, 1)):
        moves[n, 0 : COMPS * rows, :] = pltpu.roll(wide, dx % xs, 1) if dx else wide

    arrive(start_copies)
    halo[0, place_of(0, 0)] = tiles[0]
    corner = jnp.concatenate([halo[0, place_of(dz, dy)] for dz in (0, 1) for dy in (0, 1)], axis=0)
    moved[...] = dot_right(w_rise[...].astype(BF16), dot_left(corner, w_nodes[...].astype(BF16)))

    arrive(image_copies[4:6])

    def clear(dz, dy, *views):
        def run():
            for ref, index in views:
                ref[index] = jnp.zeros(ref[index].shape, F32)

        pl.when(jnp.logical_not(present(dz, dy)))(run)

    for n, d in enumerate((1, -1)):
        clear(0, d, (got_rows, (n,)))
    top = TILE + ys
    ref_ext[2 : 2 + zs, top, :] = got_rows[0, zs : 2 * zs, :]
    ref_ext[2 : 2 + zs, top + 1, :] = got_rows[0, 0:zs, :]
    def_ext[1 : 1 + zs, top, :] = got_rows[0, 2 * zs :, :]
    ref_ext[2 : 2 + zs, TILE - 2, :] = got_rows[1, 0:zs, :]
    ref_ext[2 : 2 + zs, TILE - 1, :] = got_rows[1, zs : 2 * zs, :]
    def_ext[1 : 1 + zs, TILE - 1, :] = got_rows[1, 2 * zs :, :]
    def lean(z):
        for n, dy in enumerate((-1, 1)):
            def_side[n, z] = def_ext[z, TILE + dy : TILE + dy + ys, :]

    def lean_own(z, carry):
        lean(z)
        return carry

    lax.fori_loop(1, zs + 1, lean_own, 0)

    lane = lax.broadcasted_iota(jnp.int32, (TILE, xs), 1)

    def along(value, d):
        rolled = pltpu.roll(value, (-d) % xs, 1)
        inside = lane < xs - d if d > 0 else lane >= -d
        return jnp.where(inside, rolled, 0.0)

    def moved_at(j, z, r):
        return moved[pl.ds(pl.multiple_of((j * zs + z) * ys + r * elem, elem), elem), :]

    def flat(z, carry):
        for r in range(rows):
            base = TILE + r * elem

            def ref(dy):
                return ref_ext[z + 2, base + dy : base + dy + elem, :]

            centre = ref(0)
            gy = (ref(-2) - ref(2) + 8.0 * (ref(1) - ref(-1))) * (1.0 / 12.0)
            gx = along(centre, -2) - along(centre, 2) + 8.0 * (along(centre, 1) - along(centre, -1))
            gx = gx * (1.0 / 12.0)
            here = slice(r * elem, (r + 1) * elem)
            grads[1, z, here, :] = gy
            grads[2, z, here, :] = gx
            model[z, here, :] = gy * moved_at(1, z, r) + gx * moved_at(2, z, r)
        return carry

    def deep(z, carry):
        for r in range(rows):
            base = TILE + r * elem

            def ref(dz):
                return ref_ext[z + (2 + dz), base : base + elem, :]

            gz = (ref(-2) - ref(2) + 8.0 * (ref(1) - ref(-1))) * (1.0 / 12.0)
            here = slice(r * elem, (r + 1) * elem)
            grads[0, z, here, :] = gz
            model[z, here, :] = model[z, here, :] + gz * moved_at(0, z, r)
        return carry

    def warp(z, carry):
        for r in range(rows):
            here = slice(r * elem, (r + 1) * elem)
            warped = None
            for n, dx in enumerate((-1, 0, 1)):
                s = [moves[n, j * rows + r : j * rows + r + 1, :] for j in range(2)]
                s = [jnp.broadcast_to(v, (elem, xs)) for v in s]
                below, above = s[0] < -0.5, s[0] > 0.5
                line = []
                for dy in (-1, 0, 1):

                    def layer(dz):
                        if dy == 0:
                            return def_ext[z + 1 + dz, TILE + r * elem : TILE + (r + 1) * elem, :]
                        return def_side[(dy + 1) // 2, z + 1 + dz, here, :]

                    value = jnp.where(below, layer(-1), layer(0))
                    line.append(jnp.where(above, layer(1), value))
                value = jnp.where(s[1] < -0.5, line[0], line[1])
                value = jnp.where(s[1] > 0.5, line[2], value)
                if dx:
                    value = along(value, dx)
                if warped is None:
                    warped = value
                else:
                    sx = jnp.broadcast_to(moves[1, 2 * rows + r : 2 * rows + r + 1, :], (elem, xs))
                    warped = jnp.where(sx > dx - 0.5, value, warped)
            model[z, here, :] = model[z, here, :] + warped
        return carry

    lax.fori_loop(0, zs, flat, 0)
    lax.fori_loop(1, zs - 1, warp, 0)
    lax.fori_loop(2, zs - 2, deep, 0)
    arrive(image_copies[:4] + image_copies[6:])
    clear(-1, 0, (ref_ext, (slice(0, 2),)), (def_ext, (slice(0, 1),)))
    clear(1, 0, (ref_ext, (slice(2 + zs, 4 + zs),)), (def_ext, (slice(1 + zs, 2 + zs),)))
    for n, (dz, dy) in enumerate(((1, 1), (1, -1), (-1, 1), (-1, -1))):
        clear(dz, dy, (got_diag, (n,)))
    def_ext[1 + zs, top : top + 1, :] = got_diag[0, 0:1, :]
    def_ext[1 + zs, TILE - 1 : TILE, :] = got_diag[1, 0:1, :]
    def_ext[0, top : top + 1, :] = got_diag[2, zs - 1 : zs, :]
    def_ext[0, TILE - 1 : TILE, :] = got_diag[3, zs - 1 : zs, :]
    lean(0)
    lean(zs + 1)
    warp(0, 0)
    warp(zs - 1, 0)
    for z in (0, 1, zs - 2, zs - 1):
        deep(z, 0)

    width = across
    lines = xs // width

    def gather(n, carry):
        r, c = lax.div(n, lines), lax.rem(n, lines)
        ay = pl.ds(pl.multiple_of(r * elem, elem), elem)
        ax = pl.ds(pl.multiple_of(c * width, width), width)
        sums = [[None] * 3 for _ in PAIRS]
        forces = [[None] * 2 for _ in range(COMPS)]

        def add(total, weight, value):
            if weight == 0.0:
                return total
            term = value if weight == 1.0 else weight * value
            return term if total is None else total + term

        for z in range(zs):
            w = z / elem
            g = [grads[j, z, ay, ax] for j in range(COMPS)]
            q = ref_ext[2 + z, pl.ds(pl.multiple_of(TILE + r * elem, elem), elem), ax] - model[z, ay, ax]
            model[z, ay, ax] = q
            for ij, (i, j) in enumerate(PAIRS):
                product = g[i] * g[j]
                if i == j:
                    carry = carry + product
                for cz, weight in enumerate(((1 - w) ** 2, w * (1 - w), w * w)):
                    sums[ij][cz] = add(sums[ij][cz], weight, product)
            for i in range(COMPS):
                product = g[i] * q
                for cz, weight in enumerate((1 - w, w)):
                    forces[i][cz] = add(forces[i][cz], weight, product)
        for ij in range(len(PAIRS)):
            for cz in range(3):
                at = pl.multiple_of((ij * 3 + cz) * ys + r * elem, elem)
                moments[pl.ds(at, elem), ax] = sums[ij][cz]
        for i in range(COMPS):
            for cz in range(2):
                at = pl.multiple_of((i * 2 + cz) * ys + r * elem, elem)
                loads[pl.ds(at, elem), ax] = forces[i][cz]
        return carry

    energy = lax.fori_loop(0, rows * lines, gather, jnp.zeros((elem, width), F32))
    store = pltpu.make_async_copy(model, out_mismatch, out_sem)
    store.start()
    share(0, jnp.sum(energy, axis=0, keepdims=True))
    summed = dot_left(moments[...], w_stencil[...].astype(BF16))
    send_buf[...] = dot_right(w_send[...].astype(BF16), summed)
    part_copies = []
    for n, ((start, used), to) in enumerate(zip(parts, ((1, 0), (0, 1), (1, 1)))):
        size = used if n == 0 else used + TILE
        at = pl.ds(start, size)
        part_copies.append(
            (to, remote(send_buf.at[at], got_buf.at[at], part_send.at[n], part_recv.at[n], beside(*to)))
        )
    start, used = parts[0]
    at = pl.ds(start + used, TILE)
    part_copies.append(
        ((1, 0), remote(send_buf.at[at], got_buf.at[at], part_send.at[3], part_recv.at[3], beside(1, 0)))
    )
    begin(part_copies[:1])
    load_tiles = dot_right(w_loads[...].astype(BF16), dot_left(loads[...], w_hats[...].astype(BF16)))
    for (start, used), n in zip(parts, (1, 2, 3)):
        send_buf[start + used : start + used + TILE, :across] = load_tiles[n * TILE : (n + 1) * TILE]
    begin(part_copies[1:])
    coefs[...] = dot_right(w_own[...].astype(BF16), summed)

    node_lane = lax.broadcasted_iota(jnp.int32, (TILE, across), 1)
    sub = lax.broadcasted_iota(jnp.int32, (TILE, across), 0)
    line = lax.rem(sub, rows)
    group = lax.div(sub, rows)

    def neighbour(get, dz, dy):
        centre = get(place_of(dz, 0))
        if dy == 0:
            return centre
        edge = get(place_of(dz, dy))
        inner = pltpu.roll(centre, (-dy) % TILE, 0)
        outer = pltpu.roll(edge, (dy * (rows - 1)) % TILE, 0)
        return jnp.where(line == (rows - 1 if dy > 0 else 0), outer, inner)

    def start_at(place):
        return halo[0, place]

    centre = start_at(place_of(0, 0))
    lap = 6.0 * centre - neighbour(start_at, -1, 0) - neighbour(start_at, 1, 0)
    lap = lap - neighbour(start_at, 0, -1) - neighbour(start_at, 0, 1)
    lap = lap - jnp.where(node_lane > 0, pltpu.roll(centre, 1, 1), 0.0)
    lap = lap - jnp.where(node_lane < across - 1, pltpu.roll(centre, across - 1, 1), 0.0)
    lap = jnp.where(group < COMPS, lap, 0.0)

    pass_on(0)
    arrive(part_copies)
    penalty = jnp.sum(totals(0), axis=1, keepdims=True) * (reg_weight / (devices * zs * ys * xs))
    rhs = load_tiles[0:TILE] - penalty * lap
    for start, used in parts:
        rhs = rhs + got_buf[start + used : start + used + TILE, :across]
    tiles[1] = rhs
    rhs_copies = around(1)
    begin(rhs_copies)

    coefs[...] = coefs[...] + dot_right(w_came[...].astype(BF16), got_buf[...])
    for i in range(COMPS):
        same = jnp.where(group == i, 1.0, 0.0) * penalty

        def raise_by(dz, dy, part, value):
            at = pl.ds((i * 9 + place_of(dz, dy)) * TILE, TILE)
            to = pl.ds(part * across, across)
            coefs[at, to] = coefs[at, to] + value

        raise_by(0, 0, 0, 6.0 * same)
        raise_by(0, 0, 1, jnp.where(node_lane < across - 1, -same, 0.0))
        for dz, dy in ((-1, 0), (1, 0), (0, -1), (0, 1)):
            raise_by(dz, dy, 0, -same)

    arrive(rhs_copies)
    halo[1, place_of(0, 0)] = rhs
    scale = 1.0 / (penalty * SPREAD)

    def operate(get, shift):
        out = [None] * COMPS
        back = [None] * COMPS
        for dz in (-1, 0, 1):
            for dy in (-1, 0, 1):
                v = neighbour(get, dz, dy)
                ahead = pltpu.roll(v, across - 1, 1)
                for i in range(COMPS):
                    at = pl.ds((i * 9 + place_of(dz, dy)) * TILE, TILE)
                    here, link = coefs[at, 0:across], coefs[at, across : 2 * across]
                    term = here * v + link * ahead
                    out[i] = term if out[i] is None else out[i] + term
                    term = link * v
                    back[i] = term if back[i] is None else back[i] + term
        image = jnp.zeros((TILE, across), F32)
        for i in range(COMPS):
            value = out[i] + pltpu.roll(back[i], 1, 1)
            value = value + pltpu.roll(value, TILE // 2, 0)
            value = value + pltpu.roll(value, rows, 0)
            image = jnp.where(group == i, value, image)
        return image * scale - shift * get(place_of(0, 0))

    copies = [image_copies, start_copies, part_copies, rhs_copies]

    def spread(stage, image):
        tiles[stage] = image
        listed = around(stage)
        begin(listed)
        copies.append(listed)
        return listed

    def landed(stage, listed, image):
        arrive(listed)
        halo[stage, place_of(0, 0)] = image

    def publish(stage, products):
        lines = [jnp.sum(p, axis=0, keepdims=True) for p in products]
        fill = -len(lines) % TILE
        lines += [jnp.zeros((1, across), F32)] * fill
        stacked = jnp.concatenate(lines, axis=0)
        column = jnp.sum(stacked, axis=1, keepdims=True)
        at = lax.broadcasted_iota(jnp.int32, stacked.shape, 0) == lax.broadcasted_iota(jnp.int32, stacked.shape, 1)
        share(stage, jnp.sum(jnp.where(at, column, 0.0), axis=0, keepdims=True))

    def gathered(stage, count):
        row = totals(stage)
        at = lax.broadcasted_iota(jnp.int32, row.shape, 1)
        return [jnp.sum(jnp.where(at == k, row, 0.0), axis=1, keepdims=True) for k in range(count)]

    def on(stage):
        return lambda place: halo[stage, place]

    shift = 0.25
    basis = [rhs]
    for k in range(BLOCK):
        image = operate(on(k + 1), shift)
        basis.append(image)
        if k < BLOCK - 1:
            landed(k + 2, spread(k + 2, image), image)
    count = 2 * BLOCK + 1
    publish(1, [basis[k // 2] * basis[(k + 1) // 2] for k in range(count)])
    listed = spread(BLOCK + 1, basis[BLOCK])
    pass_on(1)
    landed(BLOCK + 1, listed, basis[BLOCK])
    basis.append(operate(on(BLOCK + 1), shift))
    first = gathered(1, count)
    moved, residual, direction, past = conjugate(
        ([0.0], [1.0]), ([0.0], [1.0]), (None, None, first), shift, BLOCK, True
    )
    step = combine(moved[1], basis)
    start_poly, before, size, ratio, turns = past
    for place in range(9):
        res[place] = combine(residual[1], [halo[k + 1, place] for k in range(BLOCK + 1)])

    later = turns
    chain = [res[place_of(0, 0)]]
    chain.append(operate(lambda place: res[place], later))
    listed = spread(BLOCK + 2, chain[1])
    lift = shift - later
    powers = [start_poly]
    for k in range(BLOCK - 1):
        powers.append(plus(lifted(powers[-1]), powers[-1], lift))
    olds = [combine(p, basis) for p in powers]
    twice = before
    for k in range(BLOCK - 1):
        twice = plus(lifted(twice), twice, lift)
    last = combine(twice, basis)
    pulls = [chain[0] + ratio * olds[0], chain[1] + ratio * olds[1]]
    landed(BLOCK + 2, listed, chain[1])
    chain.append(operate(on(BLOCK + 2), later))
    listed = spread(BLOCK + 3, chain[2])
    pulls.append(chain[2] + ratio * olds[2])
    old = (last - chain[2]) / size - later * olds[2]
    landed(BLOCK + 3, listed, chain[2])
    pulls.append(operate(on(BLOCK + 3), later) + ratio * old)
    count = 2 * BLOCK
    products = [pulls[k // 2] * pulls[(k + 1) // 2] for k in range(count)]
    products += [pulls[(k + 1) // 2] * chain[k // 2] for k in range(count - 1)]
    products += [chain[k // 2] * chain[(k + 1) // 2] for k in range(count - 2)]
    publish(2, products)
    pass_on(2)
    second = gathered(2, len(products))
    seconds = (second[:count], second[count : 2 * count - 1], second[2 * count - 1 :])
    moved, _, _, _ = conjugate(([0.0], [1.0]), ([1.0], [0.0]), seconds, later, BLOCK, False)
    step = step + combine(moved[0], pulls) + combine(moved[1], chain)
    step = step * scale

    for j in range(COMPS):
        out_field[j, 0] = tiles[0, j * rows : (j + 1) * rows, :] + step[j * rows : (j + 1) * rows]
    for listed in copies:
        sent(listed)
    for stage in range(3):
        for phase in range(2):
            shared(dot_send, stage, phase)
    store.wait()


def body(slabs, planes, images, shifts, initial_displacement):
    _, zs, ys, xs = images.shape
    layers, rows, across = shifts.shape[1:]
    elem = xs // across
    assert layers == 1 and zs == elem and elem == TILE and 4 * rows == TILE
    devices = slabs * planes
    parts, arrays = matrices(elem, rows, across)
    total = parts[-1][0] + parts[-1][1] + TILE
    vmem = pl.BlockSpec(memory_space=pltpu.VMEM)
    hbm = pl.BlockSpec(memory_space=pltpu.HBM)
    stages = ITERS + 1
    dma = pltpu.SemaphoreType.DMA

    def held(*shape):
        return pltpu.VMEM(shape, F32)

    return pl.pallas_call(
        functools.partial(kernel, slabs, planes, parts),
        out_shape=(
            jax.ShapeDtypeStruct(initial_displacement.shape, F32),
            jax.ShapeDtypeStruct(images.shape[1:], F32),
        ),
        in_specs=[hbm] * (3 + len(arrays)),
        out_specs=(vmem, hbm),
        scratch_shapes=[
            held(zs + 4, ys + 2 * TILE, xs),
            held(zs + 2, ys + 2 * TILE, xs),
            held(2, zs + 2, ys, xs),
            held(2, 3 * zs, xs),
            held(2, 3 * zs, xs),
            held(4, zs, xs),
            held(stages, TILE, across),
            held(stages, 9, TILE, across),
            held(3, planes, 2, across),
            held(3, slabs, 2, across),
            held(COMPS, zs, ys, xs),
            held(zs, ys, xs),
            held(COMPS * zs * ys, xs),
            held(3, TILE, xs),
            held(len(PAIRS) * 3 * ys, xs),
            held(COMPS * 2 * ys, xs),
            held(total, 2 * across),
            held(total, 2 * across),
            held(COMPS * 9 * TILE + TILE, 2 * across),
            held(9, TILE, across),
            pltpu.VMEM(shifts.shape, jnp.int32),
            held(*initial_displacement.shape),
            *[held(*a.shape) for a in arrays],
            dma((2,)),
            dma((2 + len(arrays),)),
            dma,
            dma((2, 2)),
            dma((2, 2)),
            dma((2,)),
            dma((2,)),
            dma((4,)),
            dma((4,)),
            dma((stages, 8)),
            dma((stages, 8)),
            dma((3, 2)),
            dma((3, 2)),
            dma((4,)),
            dma((4,)),
        ],
        compiler_params=pltpu.CompilerParams(
            collective_id=0, has_side_effects=True, vmem_limit_bytes=56 * 1024 * 1024
        ),
        name="gauss_newton_step",
    )(images, shifts, initial_displacement, *[jnp.asarray(a) for a in arrays])


def solution(mesh):
    in_specs = (
        P(None, "slab", "plane", None),
        P(None, "slab", "plane", None),
        P(None, "slab", "plane", None),
    )
    out_specs = (P(None, "slab", "plane", None), P("slab", "plane", None))
    run = functools.partial(body, mesh.shape["slab"], mesh.shape["plane"])
    return jax.shard_map(run, mesh=mesh, in_specs=in_specs, out_specs=out_specs, check_vma=False)
```

```python
import functools

import jax
import jax.numpy as jnp
import numpy as np
from jax import lax
from jax.experimental import pallas as pl
from jax.experimental.pallas import tpu as pltpu
from jax.sharding import PartitionSpec as P

ITERS = 6
BLOCK = ITERS // 2
SPREAD = 128.0
reg_weight = 4.0

MESH = pl.DeviceIdType.MESH
F32 = jnp.float32
BF16 = jnp.bfloat16
TILE = 8
COMPS = 3
PAIRS = ((0, 0), (0, 1), (0, 2), (1, 1), (1, 2), (2, 2))
AROUND = tuple((dz, dy) for dz in (-1, 0, 1) for dy in (-1, 0, 1) if (dz, dy) != (0, 0))


def place_of(dz, dy):
    return (dz + 1) * 3 + dy + 1


def pair_of(i, j):
    return PAIRS.index((min(i, j), max(i, j)))


def matrices(elem, rows, across):
    w = np.arange(elem) / elem
    squares = ((1 - w) ** 2, w * (1 - w), w**2)
    count = elem * across
    hats = np.zeros((count, across))
    stencil = np.zeros((count, 2 * across))
    spread = np.zeros((across, count))
    for e in range(across):
        at = slice(e * elem, (e + 1) * elem)
        spread[e, at] = 1
        hats[at, e] = 1 - w
        stencil[at, e] += squares[0]
        if e + 1 < across:
            hats[at, e + 1] = w
            stencil[at, e + 1] += squares[2]
            stencil[at, across + e] = squares[1]

    height = rows * elem
    depth = len(PAIRS) * 3 * height

    def column(ij, cz, row):
        start = (ij * 3 + cz) * height + row * elem
        return slice(start, start + elem)

    last = rows - 1
    slab_rows = [(ij, cz, cy, r) for ij in range(6) for cz in (1, 2) for cy in range(3) for r in range(rows)]
    plane_rows = [(ij, cz, cy, last) for ij in range(6) for cz in (0, 1) for cy in (1, 2)]
    diag_rows = [(ij, cz, cy, last) for ij in range(6) for cz in (1, 2) for cy in (1, 2)]
    parts = []
    start = 0
    for listed in (slab_rows, plane_rows, diag_rows):
        used = -(-len(listed) // TILE) * TILE
        parts.append((start, used))
        start += used + TILE
    total = start
    send = np.zeros((total, depth))
    index = [{}, {}, {}]
    for part, listed in enumerate((slab_rows, plane_rows, diag_rows)):
        for n, key in enumerate(listed):
            ij, cz, cy, r = key
            send[parts[part][0] + n, column(ij, cz, r)] = squares[cy]
            index[part][key] = parts[part][0] + n

    own = np.zeros((COMPS * 9 * TILE + TILE, depth))
    came = np.zeros((COMPS * 9 * TILE + TILE, total))
    for i in range(COMPS):
        for dz in (-1, 0, 1):
            for dy in (-1, 0, 1):
                for j in range(COMPS):
                    for r in range(rows):
                        out = (i * 9 + place_of(dz, dy)) * TILE + j * rows + r
                        ij = pair_of(i, j)
                        layers = {0: ((0, 0), (-1, 2)), 1: ((0, 1),), -1: ((-1, 1),)}[dz]
                        lines = {0: ((r, 0), (r - 1, 2)), 1: ((r, 1),), -1: ((r - 1, 1),)}[dy]
                        for layer, cz in layers:
                            for line, cy in lines:
                                if layer == 0 and line >= 0:
                                    own[out, column(ij, cz, line)] = squares[cy]
                                elif layer < 0 and line >= 0:
                                    came[out, index[0][(ij, cz, cy, line)]] = 1
                                elif layer == 0:
                                    came[out, index[1][(ij, cz, cy, last)]] = 1
                                else:
                                    came[out, index[2][(ij, cz, cy, last)]] = 1

    loads = np.zeros((4 * TILE, COMPS * 2 * height))

    def line_of(i, cz, row):
        start = (i * 2 + cz) * height + row * elem
        return slice(start, start + elem)

    for i in range(COMPS):
        for r in range(rows):
            out = i * rows + r
            for cz in (0, 1):
                loads[cz * TILE + out, line_of(i, cz, r)] = 1 - w
                if r > 0:
                    loads[cz * TILE + out, line_of(i, cz, r - 1)] = w
        for cz in (0, 1):
            loads[(2 + cz) * TILE + i * rows, line_of(i, cz, last)] = w
    rise = np.zeros((COMPS, elem, height, 4 * TILE))
    for j in range(COMPS):
        for z in range(elem):
            for y in range(height):
                for dz, wz in ((0, 1 - w[z]), (1, w[z])):
                    for up, wy in ((0, 1 - w[y % elem]), (1, w[y % elem])):
                        line = y // elem + up
                        at = (dz * 2 + line // rows) * TILE + j * rows + line % rows
                        rise[j, z, y, at] += wz * wy
    rise = rise.reshape(-1, 4 * TILE)
    arrays = (stencil, hats, hats.T, spread, send, own, came, loads, rise)
    return parts, [np.asarray(a, dtype=np.float32) for a in arrays]


def split(x):
    high = x.astype(BF16)
    return high, (x - high.astype(F32)).astype(BF16)


def dot(a, b):
    return jnp.dot(a, b, preferred_element_type=F32)


def dot_left(x, exact):
    high, low = split(x)
    return dot(high, exact) + dot(low, exact)


def dot_right(exact, x):
    high, low = split(x)
    return dot(exact, high) + dot(exact, low)


def times(a, b):
    if isinstance(a, float) and a == 0.0 or isinstance(b, float) and b == 0.0:
        return 0.0
    if isinstance(a, float) and a == 1.0:
        return b
    if isinstance(b, float) and b == 1.0:
        return a
    return a * b


def total(a, b):
    if isinstance(a, float) and a == 0.0:
        return b
    if isinstance(b, float) and b == 0.0:
        return a
    return a + b


def lifted(poly):
    return [0.0] + list(poly)


def plus(a, b, factor):
    out = list(a) + [0.0] * (len(b) - len(a))
    for k, value in enumerate(b):
        out[k] = total(out[k], times(factor, value))
    return out


def product(a, b):
    out = [0.0] * (len(a) + len(b) - 1)
    for i, x in enumerate(a):
        for j, y in enumerate(b):
            out[i + j] = total(out[i + j], times(x, y))
    return out


def combine(poly, values):
    out = 0.0
    for k, value in enumerate(poly):
        if not (isinstance(value, float) and value == 0.0):
            out = total(out, times(value, values[k]))
    return out


def inner(x, y, moments):
    out = combine(product(x[0], y[0]), moments[0])
    mixed = plus(product(x[0], y[1]), product(x[1], y[0]), 1.0)
    out = total(out, combine(mixed, moments[1]))
    return total(out, combine(product(x[1], y[1]), moments[2]))


def conjugate(residual, direction, moments, shift, steps, go_on):
    moved = ([0.0], [0.0])
    norm = inner(residual, residual, moments)
    turns = 0.0
    past = None
    for k in range(steps):
        image = tuple(plus(lifted(d), d, shift) for d in direction)
        bend = inner(direction, image, moments)
        size = norm / bend
        moved = tuple(plus(m, d, size) for m, d in zip(moved, direction))
        if k == steps - 1 and not go_on:
            break
        before, old = residual, direction
        residual = tuple(plus(r, i, -size) for r, i in zip(residual, image))
        fresh = inner(residual, residual, moments)
        ratio = fresh / norm
        direction = tuple(plus(r, d, ratio) for r, d in zip(residual, direction))
        turns = total(turns, (bend / norm) * (1.0 / steps))
        norm = fresh
        past = (old[1], before[1], size, ratio, turns)
    return moved, residual, direction, past


def kernel(
    slabs,
    planes,
    parts,
    images,
    shifts_in,
    start_in,
    w_stencil_in,
    w_hats_in,
    w_nodes_in,
    w_spread_in,
    w_send_in,
    w_own_in,
    w_came_in,
    w_loads_in,
    w_rise_in,
    out_field,
    out_mismatch,
    ref_ext,
    def_ext,
    def_side,
    pack,
    got_rows,
    got_diag,
    tiles,
    halo,
    dots,
    grads,
    model,
    moved,
    moves,
    moments,
    loads,
    send_buf,
    got_buf,
    coefs,
    res,
    shifts,
    start_field,
    w_stencil,
    w_hats,
    w_nodes,
    w_spread,
    w_send,
    w_own,
    w_came,
    w_loads,
    w_rise,
    load_sem,
    const_sem,
    out_sem,
    face_send,
    face_recv,
    row_send,
    row_recv,
    diag_send,
    diag_recv,
    tile_send,
    tile_recv,
    dot_send,
    dot_recv,
    part_send,
    part_recv,
):
    _, zs, ys, xs = images.shape
    rows, across = shifts_in.shape[2], shifts_in.shape[3]
    elem = xs // across
    devices = slabs * planes
    slab, plane = lax.axis_index("slab"), lax.axis_index("plane")
    me = slab * planes + plane

    def present(dz, dy):
        ok = None
        for d, at, count in ((dz, slab, slabs), (dy, plane, planes)):
            if d:
                here = at < count - 1 if d > 0 else at > 0
                ok = here if ok is None else jnp.logical_and(ok, here)
        return ok

    def beside(dz, dy):
        return (slab + dz, plane + dy)

    plane_to = [plane] + [jnp.where(plane + k < planes, plane + k, plane + k - planes) for k in range(1, planes)]

    def everyone(action):
        for to in plane_to[1:]:
            action((slab, to))

        def there(k, carry):
            at = jnp.where(slab + k < slabs, slab + k, slab + k - slabs)
            for to in plane_to:
                action((at, to))
            return carry

        lax.fori_loop(1, slabs, there, 0)

    mine = [
        pltpu.make_async_copy(images.at[0], ref_ext.at[pl.ds(2, zs), pl.ds(TILE, ys)], load_sem.at[0]),
        pltpu.make_async_copy(images.at[1], def_ext.at[pl.ds(1, zs), pl.ds(TILE, ys)], load_sem.at[1]),
    ]
    small = [
        pltpu.make_async_copy(src, dst, const_sem.at[n])
        for n, (src, dst) in enumerate(
            (
                (start_in, start_field),
                (shifts_in, shifts),
                (w_spread_in, w_spread),
                (w_nodes_in, w_nodes),
                (w_stencil_in, w_stencil),
                (w_hats_in, w_hats),
                (w_loads_in, w_loads),
                (w_send_in, w_send),
                (w_own_in, w_own),
                (w_came_in, w_came),
                (w_rise_in, w_rise),
            )
        )
    ]
    for copy in mine + small:
        copy.start()
    halo[...] = jnp.zeros(halo.shape, F32)
    tiles[...] = jnp.zeros(tiles.shape, F32)
    got_buf[...] = jnp.zeros(got_buf.shape, F32)
    barrier = pltpu.get_barrier_semaphore()
    everyone(lambda to: pl.semaphore_signal(barrier, inc=1, device_id=to, device_id_type=MESH))
    for copy in small[:1] + mine:
        copy.wait()
    for j in range(COMPS):
        tiles[0, j * rows : (j + 1) * rows, :] = start_field[j, 0]

    for side, (far, near) in enumerate(((1, 0), (ys - 2, ys - 1))):
        pack[side, 0:zs, :] = ref_ext[2 : 2 + zs, TILE + far, :]
        pack[side, zs : 2 * zs, :] = ref_ext[2 : 2 + zs, TILE + near, :]
        pack[side, 2 * zs :, :] = def_ext[1 : 1 + zs, TILE + near, :]
    pl.semaphore_wait(barrier, devices - 1)

    def remote(src, dst, send, recv, to):
        return pltpu.make_async_remote_copy(
            src_ref=src, dst_ref=dst, send_sem=send, recv_sem=recv, device_id=to, device_id_type=MESH
        )

    def faces():
        out = []
        for n, d in enumerate((-1, 1)):
            low = 0 if d < 0 else zs - 2
            here = ref_ext.at[pl.ds(2 + low, 2), pl.ds(TILE, ys)]
            there = ref_ext.at[pl.ds(2 + zs if d < 0 else 0, 2), pl.ds(TILE, ys)]
            out.append(((d, 0), remote(here, there, face_send.at[n, 0], face_recv.at[n, 0], beside(d, 0))))
            low = 0 if d < 0 else zs - 1
            here = def_ext.at[pl.ds(1 + low, 1), pl.ds(TILE, ys)]
            there = def_ext.at[pl.ds(1 + zs if d < 0 else 0, 1), pl.ds(TILE, ys)]
            out.append(((d, 0), remote(here, there, face_send.at[n, 1], face_recv.at[n, 1], beside(d, 0))))
        for n, d in enumerate((-1, 1)):
            out.append(
                ((0, d), remote(pack.at[n], got_rows.at[n], row_send.at[n], row_recv.at[n], beside(0, d)))
            )
        for n, (dz, dy) in enumerate(((-1, -1), (-1, 1), (1, -1), (1, 1))):
            here = pack.at[(dy + 1) // 2, pl.ds(2 * zs, zs)]
            out.append(
                ((dz, dy), remote(here, got_diag.at[n], diag_send.at[n], diag_recv.at[n], beside(dz, dy)))
            )
        return out

    def around(stage):
        out = []
        for n, (dz, dy) in enumerate(AROUND):
            copy = remote(
                tiles.at[stage],
                halo.at[stage, place_of(-dz, -dy)],
                tile_send.at[stage, n],
                tile_recv.at[stage, n],
                beside(dz, dy),
            )
            out.append(((dz, dy), copy))
        return out

    def begin(copies):
        for (dz, dy), copy in copies:
            pl.when(present(dz, dy))(copy.start)

    def arrive(copies):
        for (dz, dy), copy in copies:
            pl.when(present(-dz, -dy))(copy.wait_recv)

    def sent(copies):
        for (dz, dy), copy in copies:
            pl.when(present(dz, dy))(copy.wait_send)

    def share(stage):
        slot = dots.at[stage, me]
        everyone(lambda to: remote(slot, slot, dot_send.at[stage], dot_recv.at[stage], to).start())

    def shared(sem, stage):
        some = dots.at[stage, pl.ds(0, devices - 1)]
        pltpu.make_async_copy(some, some, sem.at[stage]).wait()

    def totals(stage):
        shared(dot_recv, stage)
        lanes = jnp.sum(dots[stage], axis=0)
        return jnp.sum(lanes, axis=1, keepdims=True)

    image_copies = faces()
    start_copies = around(0)
    begin(image_copies[:4])
    begin(start_copies)
    begin(image_copies[4:])
    for copy in small[1:]:
        copy.wait()

    codes = jnp.concatenate([shifts[j, 0] for j in range(COMPS)], axis=0).astype(F32).astype(BF16)
    wide = dot(codes, w_spread[...].astype(BF16))
    for n, dx in enumerate((-1, 0, 1)):
        moves[n, 0 : COMPS * rows, :] = pltpu.roll(wide, dx % xs, 1) if dx else wide

    arrive(start_copies)
    halo[0, place_of(0, 0)] = tiles[0]
    corner = jnp.concatenate([halo[0, place_of(dz, dy)] for dz in (0, 1) for dy in (0, 1)], axis=0)
    moved[...] = dot_right(w_rise[...].astype(BF16), dot_left(corner, w_nodes[...].astype(BF16)))

    arrive(image_copies[4:6])

    def clear(dz, dy, *views):
        def run():
            for ref, index in views:
                ref[index] = jnp.zeros(ref[index].shape, F32)

        pl.when(jnp.logical_not(present(dz, dy)))(run)

    for n, d in enumerate((1, -1)):
        clear(0, d, (got_rows, (n,)))
    top = TILE + ys
    ref_ext[2 : 2 + zs, top, :] = got_rows[0, zs : 2 * zs, :]
    ref_ext[2 : 2 + zs, top + 1, :] = got_rows[0, 0:zs, :]
    def_ext[1 : 1 + zs, top, :] = got_rows[0, 2 * zs :, :]
    ref_ext[2 : 2 + zs, TILE - 2, :] = got_rows[1, 0:zs, :]
    ref_ext[2 : 2 + zs, TILE - 1, :] = got_rows[1, zs : 2 * zs, :]
    def_ext[1 : 1 + zs, TILE - 1, :] = got_rows[1, 2 * zs :, :]
    def lean(z):
        for n, dy in enumerate((-1, 1)):
            def_side[n, z] = def_ext[z, TILE + dy : TILE + dy + ys, :]

    def lean_own(z, carry):
        lean(z)
        return carry

    lax.fori_loop(1, zs + 1, lean_own, 0)

    lane = lax.broadcasted_iota(jnp.int32, (TILE, xs), 1)

    def along(value, d):
        rolled = pltpu.roll(value, (-d) % xs, 1)
        inside = lane < xs - d if d > 0 else lane >= -d
        return jnp.where(inside, rolled, 0.0)

    def moved_at(j, z, r):
        return moved[pl.ds(pl.multiple_of((j * zs + z) * ys + r * elem, elem), elem), :]

    def flat(z, carry):
        for r in range(rows):
            base = TILE + r * elem

            def ref(dy):
                return ref_ext[z + 2, base + dy : base + dy + elem, :]

            centre = ref(0)
            gy = (ref(-2) - ref(2) + 8.0 * (ref(1) - ref(-1))) * (1.0 / 12.0)
            gx = along(centre, -2) - along(centre, 2) + 8.0 * (along(centre, 1) - along(centre, -1))
            gx = gx * (1.0 / 12.0)
            here = slice(r * elem, (r + 1) * elem)
            grads[1, z, here, :] = gy
            grads[2, z, here, :] = gx
            model[z, here, :] = gy * moved_at(1, z, r) + gx * moved_at(2, z, r)
        return carry

    def deep(z, carry):
        for r in range(rows):
            base = TILE + r * elem

            def ref(dz):
                return ref_ext[z + (2 + dz), base : base + elem, :]

            gz = (ref(-2) - ref(2) + 8.0 * (ref(1) - ref(-1))) * (1.0 / 12.0)
            here = slice(r * elem, (r + 1) * elem)
            grads[0, z, here, :] = gz
            model[z, here, :] = model[z, here, :] + gz * moved_at(0, z, r)
        return carry

    def warp(z, count):
        for r in range(rows):
            here = slice(r * elem, (r + 1) * elem)
            warped = [None] * count
            for n, dx in enumerate((-1, 0, 1)):
                pieces = [[] for _ in range(count)]
                for c in range(xs // across):
                    ax = slice(c * across, (c + 1) * across)
                    s = [moves[n, j * rows + r : j * rows + r + 1, ax] for j in range(2)]
                    s = [jnp.broadcast_to(v, (elem, across)) for v in s]
                    below, above = s[0] < -0.5, s[0] > 0.5
                    left, right = s[1] < -0.5, s[1] > 0.5
                    picked = [[] for _ in range(count)]
                    for dy in (-1, 0, 1):
                        layers = []
                        for at in range(count + 2):
                            if dy == 0:
                                layers.append(def_ext[z + at, TILE + r * elem : TILE + (r + 1) * elem, ax])
                            else:
                                layers.append(def_side[(dy + 1) // 2, z + at, here, ax])
                        for k in range(count):
                            value = jnp.where(below, layers[k], layers[k + 1])
                            picked[k].append(jnp.where(above, layers[k + 2], value))
                    for k in range(count):
                        value = jnp.where(left, picked[k][0], picked[k][1])
                        pieces[k].append(jnp.where(right, picked[k][2], value))
                sx = jnp.broadcast_to(moves[1, 2 * rows + r : 2 * rows + r + 1, :], (elem, xs))
                for k in range(count):
                    value = jnp.concatenate(pieces[k], axis=1)
                    if dx:
                        value = along(value, dx)
                    warped[k] = value if n == 0 else jnp.where(sx > dx - 0.5, value, warped[k])
            for k in range(count):
                model[z + k, here, :] = model[z + k, here, :] + warped[k]

    def warp_pair(k, carry):
        warp(1 + 2 * k, 2)
        return carry

    lax.fori_loop(0, zs, flat, 0)
    lax.fori_loop(0, (zs - 2) // 2, warp_pair, 0)
    lax.fori_loop(2, zs - 2, deep, 0)
    arrive(image_copies[:4] + image_copies[6:])
    clear(-1, 0, (ref_ext, (slice(0, 2),)), (def_ext, (slice(0, 1),)))
    clear(1, 0, (ref_ext, (slice(2 + zs, 4 + zs),)), (def_ext, (slice(1 + zs, 2 + zs),)))
    for n, (dz, dy) in enumerate(((1, 1), (1, -1), (-1, 1), (-1, -1))):
        clear(dz, dy, (got_diag, (n,)))
    def_ext[1 + zs, top : top + 1, :] = got_diag[0, 0:1, :]
    def_ext[1 + zs, TILE - 1 : TILE, :] = got_diag[1, 0:1, :]
    def_ext[0, top : top + 1, :] = got_diag[2, zs - 1 : zs, :]
    def_ext[0, TILE - 1 : TILE, :] = got_diag[3, zs - 1 : zs, :]
    lean(0)
    lean(zs + 1)
    warp(0, 1)
    warp(zs - 1, 1)
    for z in (0, 1, zs - 2, zs - 1):
        deep(z, 0)

    width = across
    lines = xs // width

    def gather(n, carry):
        r, c = lax.div(n, lines), lax.rem(n, lines)
        ay = pl.ds(pl.multiple_of(r * elem, elem), elem)
        ax = pl.ds(pl.multiple_of(c * width, width), width)
        sums = [[None] * 3 for _ in PAIRS]
        forces = [[None] * 2 for _ in range(COMPS)]

        def add(total, weight, value):
            if weight == 0.0:
                return total
            term = value if weight == 1.0 else weight * value
            return term if total is None else total + term

        for z in range(zs):
            w = z / elem
            g = [grads[j, z, ay, ax] for j in range(COMPS)]
            q = ref_ext[2 + z, pl.ds(pl.multiple_of(TILE + r * elem, elem), elem), ax] - model[z, ay, ax]
            model[z, ay, ax] = q
            for ij, (i, j) in enumerate(PAIRS):
                product = g[i] * g[j]
                if i == j:
                    carry = carry + product
                for cz, weight in enumerate(((1 - w) ** 2, w * (1 - w), w * w)):
                    sums[ij][cz] = add(sums[ij][cz], weight, product)
            for i in range(COMPS):
                product = g[i] * q
                for cz, weight in enumerate((1 - w, w)):
                    forces[i][cz] = add(forces[i][cz], weight, product)
        for ij in range(len(PAIRS)):
            for cz in range(3):
                at = pl.multiple_of((ij * 3 + cz) * ys + r * elem, elem)
                moments[pl.ds(at, elem), ax] = sums[ij][cz]
        for i in range(COMPS):
            for cz in range(2):
                at = pl.multiple_of((i * 2 + cz) * ys + r * elem, elem)
                loads[pl.ds(at, elem), ax] = forces[i][cz]
        return carry

    energy = lax.fori_loop(0, rows * lines, gather, jnp.zeros((elem, width), F32))
    store = pltpu.make_async_copy(model, out_mismatch, out_sem)
    store.start()
    dots[0, me] = jnp.zeros(dots.shape[2:], F32)
    dots[0, me, 0:1, :] = jnp.sum(energy, axis=0, keepdims=True)
    share(0)
    summed = dot_left(moments[...], w_stencil[...].astype(BF16))
    send_buf[...] = dot_right(w_send[...].astype(BF16), summed)
    part_copies = []
    for n, ((start, used), to) in enumerate(zip(parts, ((1, 0), (0, 1), (1, 1)))):
        size = used if n == 0 else used + TILE
        at = pl.ds(start, size)
        part_copies.append(
            (to, remote(send_buf.at[at], got_buf.at[at], part_send.at[n], part_recv.at[n], beside(*to)))
        )
    start, used = parts[0]
    at = pl.ds(start + used, TILE)
    part_copies.append(
        ((1, 0), remote(send_buf.at[at], got_buf.at[at], part_send.at[3], part_recv.at[3], beside(1, 0)))
    )
    begin(part_copies[:1])
    load_tiles = dot_right(w_loads[...].astype(BF16), dot_left(loads[...], w_hats[...].astype(BF16)))
    for (start, used), n in zip(parts, (1, 2, 3)):
        send_buf[start + used : start + used + TILE, :across] = load_tiles[n * TILE : (n + 1) * TILE]
    begin(part_copies[1:])
    coefs[...] = dot_right(w_own[...].astype(BF16), summed)

    node_lane = lax.broadcasted_iota(jnp.int32, (TILE, across), 1)
    sub = lax.broadcasted_iota(jnp.int32, (TILE, across), 0)
    line = lax.rem(sub, rows)
    group = lax.div(sub, rows)

    def neighbour(get, dz, dy):
        centre = get(place_of(dz, 0))
        if dy == 0:
            return centre
        edge = get(place_of(dz, dy))
        inner = pltpu.roll(centre, (-dy) % TILE, 0)
        outer = pltpu.roll(edge, (dy * (rows - 1)) % TILE, 0)
        return jnp.where(line == (rows - 1 if dy > 0 else 0), outer, inner)

    def start_at(place):
        return halo[0, place]

    centre = start_at(place_of(0, 0))
    lap = 6.0 * centre - neighbour(start_at, -1, 0) - neighbour(start_at, 1, 0)
    lap = lap - neighbour(start_at, 0, -1) - neighbour(start_at, 0, 1)
    lap = lap - jnp.where(node_lane > 0, pltpu.roll(centre, 1, 1), 0.0)
    lap = lap - jnp.where(node_lane < across - 1, pltpu.roll(centre, across - 1, 1), 0.0)
    lap = jnp.where(group < COMPS, lap, 0.0)

    penalty = totals(0)[0:1, :] * (reg_weight / (devices * zs * ys * xs))
    arrive(part_copies)
    rhs = load_tiles[0:TILE] - penalty * lap
    for start, used in parts:
        rhs = rhs + got_buf[start + used : start + used + TILE, :across]
    tiles[1] = rhs
    rhs_copies = around(1)
    begin(rhs_copies)

    coefs[...] = coefs[...] + dot_right(w_came[...].astype(BF16), got_buf[...])
    for i in range(COMPS):
        same = jnp.where(group == i, 1.0, 0.0) * penalty

        def raise_by(dz, dy, part, value):
            at = pl.ds((i * 9 + place_of(dz, dy)) * TILE, TILE)
            to = pl.ds(part * across, across)
            coefs[at, to] = coefs[at, to] + value

        raise_by(0, 0, 0, 6.0 * same)
        raise_by(0, 0, 1, jnp.where(node_lane < across - 1, -same, 0.0))
        for dz, dy in ((-1, 0), (1, 0), (0, -1), (0, 1)):
            raise_by(dz, dy, 0, -same)

    arrive(rhs_copies)
    halo[1, place_of(0, 0)] = rhs
    scale = 1.0 / (penalty * SPREAD)

    def operate(get, shift):
        out = [None] * COMPS
        back = [None] * COMPS
        for dz in (-1, 0, 1):
            for dy in (-1, 0, 1):
                v = neighbour(get, dz, dy)
                ahead = pltpu.roll(v, across - 1, 1)
                for i in range(COMPS):
                    at = pl.ds((i * 9 + place_of(dz, dy)) * TILE, TILE)
                    here, link = coefs[at, 0:across], coefs[at, across : 2 * across]
                    term = here * v + link * ahead
                    out[i] = term if out[i] is None else out[i] + term
                    term = link * v
                    back[i] = term if back[i] is None else back[i] + term
        image = jnp.zeros((TILE, across), F32)
        for i in range(COMPS):
            value = out[i] + pltpu.roll(back[i], 1, 1)
            value = value + pltpu.roll(value, TILE // 2, 0)
            value = value + pltpu.roll(value, rows, 0)
            image = jnp.where(group == i, value, image)
        return image * scale - shift * get(place_of(0, 0))

    copies = [image_copies, start_copies, part_copies, rhs_copies]

    def spread(stage, image):
        tiles[stage] = image
        listed = around(stage)
        begin(listed)
        copies.append(listed)
        return listed

    def landed(stage, listed, image):
        arrive(listed)
        halo[stage, place_of(0, 0)] = image

    def publish(stage, products):
        lines = [jnp.sum(p, axis=0, keepdims=True) for p in products]
        fill = -len(lines) % TILE
        lines += [jnp.zeros((1, across), F32)] * fill
        stacked = jnp.concatenate(lines, axis=0)
        column = jnp.sum(stacked, axis=1, keepdims=True)
        at = lax.broadcasted_iota(jnp.int32, stacked.shape, 0) == lax.broadcasted_iota(jnp.int32, stacked.shape, 1)
        dots[stage, me] = jnp.zeros(dots.shape[2:], F32)
        dots[stage, me, 0:1, :] = jnp.sum(jnp.where(at, column, 0.0), axis=0, keepdims=True)
        share(stage)

    def gathered(stage, count):
        shared(dot_recv, stage)
        row = jnp.sum(dots[stage], axis=0)[0:1, :]
        at = lax.broadcasted_iota(jnp.int32, row.shape, 1)
        return [jnp.sum(jnp.where(at == k, row, 0.0), axis=1, keepdims=True) for k in range(count)]

    def on(stage):
        return lambda place: halo[stage, place]

    shift = 0.25
    basis = [rhs]
    for k in range(BLOCK):
        image = operate(on(k + 1), shift)
        basis.append(image)
        if k < BLOCK - 1:
            landed(k + 2, spread(k + 2, image), image)
    count = 2 * BLOCK + 1
    publish(1, [basis[k // 2] * basis[(k + 1) // 2] for k in range(count)])
    listed = spread(BLOCK + 1, basis[BLOCK])
    landed(BLOCK + 1, listed, basis[BLOCK])
    basis.append(operate(on(BLOCK + 1), shift))
    first = gathered(1, count)
    moved, residual, direction, past = conjugate(
        ([0.0], [1.0]), ([0.0], [1.0]), (None, None, first), shift, BLOCK, True
    )
    step = combine(moved[1], basis)
    start_poly, before, size, ratio, turns = past
    for place in range(9):
        res[place] = combine(residual[1], [halo[k + 1, place] for k in range(BLOCK + 1)])

    later = turns
    chain = [res[place_of(0, 0)]]
    chain.append(operate(lambda place: res[place], later))
    listed = spread(BLOCK + 2, chain[1])
    lift = shift - later
    powers = [start_poly]
    for k in range(BLOCK - 1):
        powers.append(plus(lifted(powers[-1]), powers[-1], lift))
    olds = [combine(p, basis) for p in powers]
    twice = before
    for k in range(BLOCK - 1):
        twice = plus(lifted(twice), twice, lift)
    last = combine(twice, basis)
    pulls = [chain[0] + ratio * olds[0], chain[1] + ratio * olds[1]]
    landed(BLOCK + 2, listed, chain[1])
    chain.append(operate(on(BLOCK + 2), later))
    listed = spread(BLOCK + 3, chain[2])
    pulls.append(chain[2] + ratio * olds[2])
    old = (last - chain[2]) / size - later * olds[2]
    landed(BLOCK + 3, listed, chain[2])
    pulls.append(operate(on(BLOCK + 3), later) + ratio * old)
    count = 2 * BLOCK
    products = [pulls[k // 2] * pulls[(k + 1) // 2] for k in range(count)]
    products += [pulls[(k + 1) // 2] * chain[k // 2] for k in range(count - 1)]
    products += [chain[k // 2] * chain[(k + 1) // 2] for k in range(count - 2)]
    publish(2, products)
    second = gathered(2, len(products))
    seconds = (second[:count], second[count : 2 * count - 1], second[2 * count - 1 :])
    moved, _, _, _ = conjugate(([0.0], [1.0]), ([1.0], [0.0]), seconds, later, BLOCK, False)
    step = step + combine(moved[0], pulls) + combine(moved[1], chain)
    step = step * scale

    for j in range(COMPS):
        out_field[j, 0] = tiles[0, j * rows : (j + 1) * rows, :] + step[j * rows : (j + 1) * rows]
    for listed in copies:
        sent(listed)
    for stage in range(3):
        shared(dot_send, stage)
    store.wait()


def body(slabs, planes, images, shifts, initial_displacement):
    _, zs, ys, xs = images.shape
    layers, rows, across = shifts.shape[1:]
    elem = xs // across
    assert layers == 1 and zs == elem and elem == TILE and 4 * rows == TILE
    devices = slabs * planes
    parts, arrays = matrices(elem, rows, across)
    total = parts[-1][0] + parts[-1][1] + TILE
    vmem = pl.BlockSpec(memory_space=pltpu.VMEM)
    hbm = pl.BlockSpec(memory_space=pltpu.HBM)
    stages = ITERS + 1
    dma = pltpu.SemaphoreType.DMA

    def held(*shape):
        return pltpu.VMEM(shape, F32)

    return pl.pallas_call(
        functools.partial(kernel, slabs, planes, parts),
        out_shape=(
            jax.ShapeDtypeStruct(initial_displacement.shape, F32),
            jax.ShapeDtypeStruct(images.shape[1:], F32),
        ),
        in_specs=[hbm] * (3 + len(arrays)),
        out_specs=(vmem, hbm),
        scratch_shapes=[
            held(zs + 4, ys + 2 * TILE, xs),
            held(zs + 2, ys + 2 * TILE, xs),
            held(2, zs + 2, ys, xs),
            held(2, 3 * zs, xs),
            held(2, 3 * zs, xs),
            held(4, zs, xs),
            held(stages, TILE, across),
            held(stages, 9, TILE, across),
            held(3, devices, 2, across),
            held(COMPS, zs, ys, xs),
            held(zs, ys, xs),
            held(COMPS * zs * ys, xs),
            held(3, TILE, xs),
            held(len(PAIRS) * 3 * ys, xs),
            held(COMPS * 2 * ys, xs),
            held(total, 2 * across),
            held(total, 2 * across),
            held(COMPS * 9 * TILE + TILE, 2 * across),
            held(9, TILE, across),
            pltpu.VMEM(shifts.shape, jnp.int32),
            held(*initial_displacement.shape),
            *[held(*a.shape) for a in arrays],
            dma((2,)),
            dma((2 + len(arrays),)),
            dma,
            dma((2, 2)),
            dma((2, 2)),
            dma((2,)),
            dma((2,)),
            dma((4,)),
            dma((4,)),
            dma((stages, 8)),
            dma((stages, 8)),
            dma((3,)),
            dma((3,)),
            dma((4,)),
            dma((4,)),
        ],
        compiler_params=pltpu.CompilerParams(
            collective_id=0, has_side_effects=True, vmem_limit_bytes=56 * 1024 * 1024
        ),
        name="gauss_newton_step",
    )(images, shifts, initial_displacement, *[jnp.asarray(a) for a in arrays])


def solution(mesh):
    in_specs = (
        P(None, "slab", "plane", None),
        P(None, "slab", "plane", None),
        P(None, "slab", "plane", None),
    )
    out_specs = (P(None, "slab", "plane", None), P("slab", "plane", None))
    run = functools.partial(body, mesh.shape["slab"], mesh.shape["plane"])
    return jax.shard_map(run, mesh=mesh, in_specs=in_specs, out_specs=out_specs, check_vma=False)
```
